32 devices in a mesh: gx: 2 (over y), gy: 4 (over x, core), gz: 4 (over z).
Axes of the slice: x: 2, y: 2, z: 4, core: 2. Of those that a mesh axis runs over, the one named last changes fastest.
Arguments:
- fields: float32 [6, 32, 64, 512], P(None, 'gx', 'gy', 'gz'), may hold values from -6 to 6
- polarization: float32 [6, 32, 64, 512], P(None, 'gx', 'gy', 'gz'), may hold values from -3 to 3
- material: int32 [32, 64, 512], P('gx', 'gy', 'gz'), may hold values from 0 to 4
- omega0: float32 [4], replicated, may hold values from 0.1 to 0.5
- damping: float32 [4], replicated, may hold values from 0.05 to 0.8
- strength: float32 [4], replicated, may hold values from 0.5 to 2.5
- tile_count: int32 [8, 4], P(('gx', 'gy')), may hold values from 1 to 18, 24 in all within a row
- tile_place: int32 [8, 4, 18], P(('gx', 'gy')), may hold values from 0 to 31, as said below
- dir_angles: float32 [2, 8192], replicated, may hold values from 0 to 3.14159
- dir_order: int32 [8192], replicated, may hold values from 0 to 8191, each once
Outputs:
- fields_out: float32 [6, 32, 64, 512], P(None, 'gx', 'gy', 'gz')
- far_field: float32 [8192, 8], P(('gx', 'gy', 'gz'))
The draws below stay inside these ranges and needn't reach their ends.
Inputs may be any that keep to these rules, and one draw needn't show every extreme that they name: `tile_count`: for each column g, the 4 counts sum to 24, and the largest of them is exactly 18. `tile_place`: the 18 positions of one device are distinct; only the first tile_count of them are live tiles.
All inputs are finite; a program needn't handle non-finite values.
Results may differ from the reference program's by a relative error of at most 0.0032.
Values may be sent and summed in bfloat16 or wider, within the bound.
A program may use at most 64 MiB of HBM per device.

```python
import math
import jax
import jax.numpy as jnp
import numpy as np
from jax import lax

CX = 16
CY = 16
CZ = 128
TY = 8
MATS = 4
STEPS = 4
DIRS = 8192
TILE_MEAN = 6
TILE_MOST = 18
NX = 32
NY = 64
NZ = 512
GROUPS = 8
GROUP_TILES = 24
TILES_ALL = 192
N_GY = 4
N_GZ = 4


def draw_tile_place(key, part):
    positions = CX * (CY // TY)
    layers = GROUP_TILES // TILE_MEAN
    row_total = GROUPS * layers
    scores = jax.random.randint(key, (row_total, positions), 0, 1 << 16) * positions + jnp.arange(positions)[None, :]
    chosen = jnp.argsort(scores, axis=1)[:, :TILE_MOST]
    return chosen.reshape(GROUPS, layers, TILE_MOST).astype(jnp.int32)


def set_ends(array, own_key, low, top_value):
    dims = array.shape
    spot = [jax.random.randint(jax.random.fold_in(own_key, axis), (), 0, dims[axis]) for axis in range(len(dims))]
    array = array.at[tuple(spot)].set(low)
    longest = dims.index(max(dims))
    spot[longest] = (spot[longest] + 1) % dims[longest]
    return array.at[tuple(spot)].set(top_value)


def block_levels(key, shape, shards, least, top_value):
    gain, own = 1.0, jax.random.fold_in(key, 6)
    for dim, blocks in shards:
        steps = jnp.exp(jax.random.uniform(jax.random.fold_in(own, dim), (blocks,), jnp.float32, least / len(shards), top_value / len(shards)))
        gain = gain * jnp.repeat(steps, shape[dim] // blocks).reshape([-1 if axis == dim else 1 for axis in range(len(shape))])
    return gain


def split_up(count, total, reach, skew):
    weights = [(1 << 20) // math.isqrt(rank ** skew) + 1 for rank in range(2, count + 1)]
    spare, given = total - reach - (count - 1), [1] * (count - 1)
    while spare > 0:
        movable = [i for i in range(count - 1) if given[i] < reach]
        pool, left = sum([weights[i] for i in movable]), spare
        for i in movable:
            extra = min(reach - given[i], max(1, left * weights[i] // pool), spare)
            given[i] = given[i] + extra
            spare = spare - extra
    return np.array([reach] + given)


def ragged_sizes(stream_key, number_of, total, reach, slope):
    if number_of == 2:
        one = jax.random.randint(stream_key, (), max(1, total - reach), min(reach, total - 1) + 1)
        return jnp.stack([one, total - one])
    sizes = jnp.asarray(split_up(number_of, total, reach, slope), jnp.int32)
    pairs = (number_of - 1) // 2
    source_of, sink = sizes[1:1 + 2 * pairs:2], sizes[2:2 + 2 * pairs:2]
    margin = jnp.minimum(source_of - 1, reach - sink)
    shifted = jax.random.randint(jax.random.fold_in(stream_key, 1), (pairs,), 0, 1 << 20) % (margin + 1)
    sizes = sizes.at[1:1 + 2 * pairs:2].set(source_of - shifted).at[2:2 + 2 * pairs:2].set(sink + shifted)
    return sizes[jax.random.permutation(jax.random.fold_in(stream_key, 2), number_of)]


def bell_draw(key, shape, width, reach, shards=(), kind=jnp.bfloat16):
    entries = width * jax.random.normal(key, shape, jnp.float32)
    if shards:
        entries = entries * block_levels(key, shape, shards, -0.22, 0.18)
    return jnp.clip(entries, -reach, reach).astype(kind)


def setup_inputs(seed: int = 0) -> dict:
    seeds = jax.random.split(jax.random.key(seed), 11)
    return {
        "fields": bell_draw(seeds[0], (6, NX, NY, NZ), 1.0, 6.0, ((1, 2), (2, 4), (3, 4)), jnp.float32),
        "polarization": bell_draw(seeds[1], (6, NX, NY, NZ), 0.5, 3.0, ((1, 2), (2, 4), (3, 4)), jnp.float32),
        "material": set_ends(jax.random.randint(seeds[2], (NX, NY, NZ), 0, MATS + 1), jax.random.fold_in(seeds[2], 1), 0, MATS).astype(jnp.int32),
        "omega0": jnp.clip(jnp.exp(jax.random.uniform(seeds[3], (MATS,), jnp.float32, math.log(0.1), math.log(0.5))), 0.1, 0.5),
        "damping": jnp.clip(jnp.exp(jax.random.uniform(seeds[4], (MATS,), jnp.float32, math.log(0.05), math.log(0.8))), 0.05, 0.8),
        "strength": jnp.clip(jax.random.uniform(seeds[5], (MATS,), jnp.float32, 0.5, 2.5), 0.5, 2.5),
        "tile_count": jax.vmap(lambda own: ragged_sizes(own, N_GZ, GROUP_TILES, TILE_MOST, 2))(jax.random.split(seeds[6], GROUPS)).reshape((GROUPS, N_GZ)).astype(jnp.int32),
        "tile_place": draw_tile_place(jax.random.fold_in(seeds[10], 71), 0),
        "dir_angles": jnp.clip(jax.random.uniform(seeds[8], (2, DIRS), jnp.float32, 0.0, 3.14159), 0.0, 3.14159),
        "dir_order": jax.random.permutation(seeds[9], DIRS).astype(jnp.int32),
    }


SPEED = 0.5
WAVE = 0.35

def lorentz(omega0, damping, strength):
    denominator = 1.0 + 0.5 * damping
    square = omega0 * omega0
    return ((2.0 - square) / denominator, -(1.0 - 0.5 * damping) / denominator, strength * square / denominator)

def lookup(material, coef_table):
    result = jnp.zeros(material.shape, jnp.float32)
    for mat_index in range(coef_table.shape[0]):
        result = result + jnp.where(material == mat_index + 1, coef_table[mat_index], 0.0)
    return result

def ahead(values, axis_id):
    extent = values.shape[axis_id]
    padded = jnp.pad(values, [(0, 1) if other == axis_id else (0, 0) for other in range(values.ndim)])
    return lax.slice_in_dim(padded, 1, extent + 1, axis=axis_id)

def behind(values, axis_id):
    extent = values.shape[axis_id]
    padded = jnp.pad(values, [(1, 0) if other == axis_id else (0, 0) for other in range(values.ndim)])
    return lax.slice_in_dim(padded, 0, extent, axis=axis_id)

def magnetic_update(electric, magnetic):
    electric_x, electric_y, electric_z = (electric[0], electric[1], electric[2])
    magnetic_x = magnetic[0] - SPEED * (ahead(electric_z, 1) - electric_z - (ahead(electric_y, 2) - electric_y))
    magnetic_y = magnetic[1] - SPEED * (ahead(electric_x, 2) - electric_x - (ahead(electric_z, 0) - electric_z))
    magnetic_z = magnetic[2] - SPEED * (ahead(electric_y, 0) - electric_y - (ahead(electric_x, 1) - electric_x))
    return jnp.stack([magnetic_x, magnetic_y, magnetic_z])

def curl_back(magnetic):
    magnetic_x, magnetic_y, magnetic_z = (magnetic[0], magnetic[1], magnetic[2])
    curl_x = magnetic_z - behind(magnetic_z, 1) - (magnetic_y - behind(magnetic_y, 2))
    curl_y = magnetic_x - behind(magnetic_x, 2) - (magnetic_z - behind(magnetic_z, 0))
    curl_z = magnetic_y - behind(magnetic_y, 0) - (magnetic_x - behind(magnetic_x, 1))
    return jnp.stack([curl_x, curl_y, curl_z])

def far_block(currents, tile_x, tile_y, tile_z, directions, rows_y, depth_z):
    row_pos = jnp.arange(rows_y, dtype=jnp.float32)
    depth_pos = jnp.arange(depth_z, dtype=jnp.float32)
    phases = WAVE * (directions[1][None, None, :] * row_pos[:, None, None] + directions[2][None, None, :] * depth_pos[None, :, None])
    phase_table = jnp.concatenate([jnp.cos(phases), jnp.sin(phases)], axis=2).astype(jnp.bfloat16)
    block_width = directions.shape[1]
    phase_table = phase_table.reshape(rows_y * depth_z, 2 * block_width)
    tiles = currents.shape[0]
    products = jnp.dot(currents.reshape(tiles * 8, rows_y * depth_z).astype(jnp.float32), phase_table.astype(jnp.float32), precision=lax.Precision.HIGHEST)
    products = products.reshape(tiles, 4, 2, 2, block_width)
    real_part = products[:, :, 0, 0] - products[:, :, 1, 1]
    imag_part = products[:, :, 0, 1] + products[:, :, 1, 0]
    tile_phase = WAVE * (directions[0][None, :] * tile_x[:, None] + directions[1][None, :] * tile_y[:, None] + directions[2][None, :] * tile_z[:, None])
    tile_cos = jnp.cos(tile_phase)[:, None, :]
    tile_sin = jnp.sin(tile_phase)[:, None, :]
    far_real = lax.optimization_barrier(jnp.sum(real_part * tile_cos - imag_part * tile_sin, axis=0))
    far_imag = lax.optimization_barrier(jnp.sum(real_part * tile_sin + imag_part * tile_cos, axis=0))
    return jnp.stack([far_real, far_imag], axis=1).reshape(8, block_width)

def reference(fields, polarization, material, omega0, damping, strength, tile_count, tile_place, dir_angles, dir_order):
    table_a, table_b, table_c = lorentz(omega0, damping, strength)
    coef_a = lookup(material, table_a)
    coef_b = lookup(material, table_b)
    coef_c = lookup(material, table_c)
    sheet_mask = jnp.where(material > 0, 1.0, 0.0).astype(jnp.float32)
    electric = fields[0:3]
    magnetic = fields[3:6]
    pol_now = polarization[0:3]
    pol_old = polarization[3:6]
    empty_sum = jnp.zeros((2,) + material.shape, jnp.float32)
    ele_real, ele_imag, mag_real, mag_imag = (empty_sum, empty_sum, empty_sum, empty_sum)
    for instant in range(STEPS):
        magnetic = magnetic_update(electric, magnetic)
        saturation = 1.0 / (1.0 + electric[0] * electric[0] + electric[1] * electric[1] + electric[2] * electric[2])
        pol_new = coef_a * pol_now + coef_b * pol_old + coef_c * saturation * electric
        electric = electric + SPEED * curl_back(magnetic) - sheet_mask * (pol_new - pol_now)
        pol_old = pol_now
        pol_now = pol_new
        angle_h = WAVE * SPEED * (instant + 0.5)
        angle_e = WAVE * SPEED * (instant + 1.0)
        mag_real = mag_real + math.cos(angle_h) * magnetic[1:3]
        mag_imag = mag_imag - math.sin(angle_h) * magnetic[1:3]
        ele_real = ele_real + math.cos(angle_e) * electric[1:3]
        ele_imag = ele_imag - math.sin(angle_e) * electric[1:3]
    fields_out = jnp.concatenate([electric, magnetic], axis=0)
    currents = jnp.stack([-mag_real[1], -mag_imag[1], mag_real[0], mag_imag[0], ele_real[1], ele_imag[1], -ele_real[0], -ele_imag[0]])
    blocks_y = CY // TY
    run_ends = jnp.cumsum(tile_count, axis=1).astype(jnp.int32)
    starts = run_ends - tile_count
    rank_ids = jnp.arange(GROUP_TILES, dtype=jnp.int32)
    source = lax.optimization_barrier(jnp.sum((run_ends[:, None, :] <= rank_ids[None, :, None]).astype(jnp.int32), axis=2))
    within = rank_ids[None, :] - jnp.take_along_axis(starts, source, axis=1)
    group_ids = jnp.broadcast_to(jnp.arange(GROUPS, dtype=jnp.int32)[:, None], source.shape)
    places = tile_place[group_ids, source, within]
    tile_x = (group_ids // N_GY * CX + places // blocks_y).reshape(-1).astype(jnp.int32)
    tile_y = (group_ids % N_GY * CY + places % blocks_y * TY).reshape(-1).astype(jnp.int32)
    tile_z = (source * CZ).reshape(-1).astype(jnp.int32)

    def cut_patch(x_start, y_start, z_start):
        patch = lax.dynamic_slice(currents, (jnp.int32(0), x_start, y_start, z_start), (8, 1, TY, CZ))
        return patch.reshape(8, TY * CZ)
    patches = jax.vmap(cut_patch)(tile_x, tile_y, tile_z).astype(jnp.bfloat16)
    polar_angle = jnp.take(dir_angles[0], dir_order)
    azimuth = jnp.take(dir_angles[1], dir_order)
    dir_vec = jnp.stack([jnp.sin(polar_angle) * jnp.cos(azimuth), jnp.sin(polar_angle) * jnp.sin(azimuth), jnp.cos(polar_angle)])
    block_width = math.gcd(DIRS, 512)
    pos_x = tile_x.astype(jnp.float32)
    pos_y = tile_y.astype(jnp.float32)
    pos_z = tile_z.astype(jnp.float32)

    def block_far(offset):
        directions = lax.dynamic_slice_in_dim(dir_vec, offset, block_width, 1)
        return far_block(patches, pos_x, pos_y, pos_z, directions, TY, CZ)
    far_blocks = lax.map(block_far, jnp.arange(DIRS // block_width, dtype=jnp.int32) * block_width)
    norm_scale = 1.0 / math.sqrt(TILES_ALL * TY * CZ)
    far_field = far_blocks.transpose(0, 2, 1).reshape(DIRS, 8) * norm_scale
    return (fields_out, far_field)
```

```python
import functools
import math

import jax
import jax.numpy as jnp
from jax import lax
from jax.experimental import pallas as pl
from jax.experimental.pallas import tpu as pltpu
from jax.sharding import PartitionSpec as P

TY = 8
STEPS = 4
TILE_MEAN = 6
SPEED = 0.5
WAVE = 0.35
LANES = 128
MESH = pl.DeviceIdType.MESH

SIN_TERMS = (
    6.283185302511505, -41.34170040531808, 81.60513138582216, -76.70301535428969,
    42.02592698929055, -14.899846680245616, 3.238137526404064,
)
COS_TERMS = (
    0.9999999890590243, -19.73920449945407, 64.93911745990263, -85.45013953100009,
    60.16763095180868, -25.967599251355935, 6.528658164931359,
)


def poly(s, terms):
    total = jnp.full_like(s, terms[-1])
    for term in terms[-2::-1]:
        total = total * s + term
    return total


def cos_sin(turns):
    t = turns - jnp.round(turns)
    s = t * t
    return poly(s, COS_TERMS), t * poly(s, SIN_TERMS)


def pick(step, values):
    result = jnp.float32(values[-1])
    for index in range(len(values) - 2, -1, -1):
        result = jnp.where(step == index, jnp.float32(values[index]), result)
    return result


def kernel(
    sizes, slots, rows,
    fields_ref, pol_ref, mat_ref, omega_ref, damp_ref, strength_ref, count_ref, place_ref,
    angles_ref, order_ref,
    out_ref, far_ref,
    ele, mag, pq, coef, acc, cur, coords, dirs, table, blocks, landed,
    e_x, e_y, e_z, h_x, h_y, h_z, sx, sy, sz,
    face_send, face_recv, pair_send, pair_recv, far_send, far_recv,
):
    n_x, n_y, n_z = sizes
    half_y = n_y // 2
    owners = n_x * half_y * n_z
    width_x, width_y, depth_z = mat_ref.shape
    blocks_y = width_y // TY
    reach = rows // 2
    ix, iy, iz = lax.axis_index("gx"), lax.axis_index("gy"), lax.axis_index("gz")
    parity = lax.rem(iy, 2)
    me = (ix * half_y + iy // 2) * n_z + iz
    place_in = (("gx", ix, n_x), ("gy", iy, n_y), ("gz", iz, n_z))

    def owner_device(m):
        return {
            "gx": m // (half_y * n_z),
            "gy": lax.rem(m // n_z, half_y) * 2 + parity,
            "gz": lax.rem(m, n_z),
        }

    for ghost in (e_x, e_y, e_z, h_x, h_y, h_z):
        ghost[...] = jnp.zeros_like(ghost)

    barrier = pltpu.get_barrier_semaphore()

    def greet(o, carry):
        pl.semaphore_signal(
            barrier, inc=1, device_id=owner_device(lax.rem(me + o, owners)), device_id_type=MESH
        )
        return carry

    lax.fori_loop(1, owners, greet, 0)

    @pl.when(iy > 0)
    def _():
        pl.semaphore_signal(barrier, inc=1, device_id={"gy": iy - 1}, device_id_type=MESH)

    @pl.when(iy < n_y - 1)
    def _():
        pl.semaphore_signal(barrier, inc=1, device_id={"gy": iy + 1}, device_id_type=MESH)

    for c in range(3):
        ele[c, pl.ds(0, width_x)] = fields_ref[c]
        mag[c, pl.ds(1, width_x)] = fields_ref[3 + c]
        pq[0, c] = pol_ref[c]
        pq[1, c] = pol_ref[3 + c]
    material = mat_ref[...]
    coefs = [jnp.zeros(material.shape, jnp.float32) for _ in range(3)]
    for m in range(omega_ref.shape[0]):
        w, g, s = omega_ref[m], damp_ref[m], strength_ref[m]
        w, g, s = (jnp.full((1, 1, depth_z), v, jnp.float32) for v in (w, g, s))
        below = 1.0 + 0.5 * g
        chosen = material == m + 1
        for i, v in enumerate(((2.0 - w * w) / below, -(1.0 - 0.5 * g) / below, s * (w * w) / below)):
            coefs[i] = jnp.where(chosen, v, coefs[i])
    for i in range(3):
        coef[i] = coefs[i]
    coef[3] = jnp.where(material > 0, 1.0, 0.0).astype(jnp.float32)

    first_x, first_y, first_z = ix * width_x, iy * width_y, iz * depth_z
    lane = lax.broadcasted_iota(jnp.int32, (1, LANES), 1)
    coords[0] = jnp.zeros(coords.shape[1:], jnp.float32)
    for j in range(slots):
        p = place_ref[0, iz, j]
        x0 = (first_x + p // blocks_y).astype(jnp.float32)
        y0 = (first_y + lax.rem(p, blocks_y) * TY).astype(jnp.float32)
        z0 = first_z.astype(jnp.float32)
        live = jnp.where(j < count_ref[0, iz], jnp.float32(1.0), jnp.float32(0.0))
        row = jnp.where(lane == 0, x0, 0.0) + jnp.where(lane == 1, y0, 0.0)
        row = row + jnp.where(lane == 2, z0, 0.0) + jnp.where(lane == 3, live, 0.0)
        coords[0, j : j + 1, :] = row

    whole = angles_ref[...]
    part_a = whole.astype(jnp.bfloat16)
    left = whole - part_a.astype(jnp.float32)
    part_b = left.astype(jnp.bfloat16)
    part_c = (left - part_b.astype(jnp.float32)).astype(jnp.bfloat16)
    parts = jnp.concatenate([part_a, part_b, part_c], axis=0)
    high_count = whole.shape[1]

    pl.semaphore_wait(
        barrier,
        owners - 1 + jnp.where(iy > 0, 1, 0) + jnp.where(iy < n_y - 1, 1, 0),
    )

    per_turn = WAVE / (2.0 * math.pi)

    def build(m, carry):
        chosen = order_ref[m // n_z, parity, lax.rem(m, n_z)]
        high = lax.broadcasted_iota(jnp.int32, (high_count, reach), 0)
        low = lax.broadcasted_iota(jnp.int32, (LANES, reach), 0)
        hot = jnp.where(high == chosen // LANES, 1.0, 0.0).astype(jnp.bfloat16)
        found = jnp.dot(parts, hot, preferred_element_type=jnp.float32)
        third = 2 * LANES
        found = found[:third] + found[third : 2 * third] + found[2 * third :]
        own = low == lax.rem(chosen, LANES)
        theta = jnp.sum(jnp.where(own, found[:LANES], 0.0), axis=0, keepdims=True)
        phi = jnp.sum(jnp.where(own, found[LANES:], 0.0), axis=0, keepdims=True)
        ct, st = cos_sin(theta * (1.0 / (2.0 * math.pi)))
        cp, sp = cos_sin(phi * (1.0 / (2.0 * math.pi)))
        ux, uy, uz = st * cp * per_turn, st * sp * per_turn, ct * per_turn
        dirs[m, 0:1, :] = ux
        dirs[m, 1:2, :] = uy
        dirs[m, 2:3, :] = uz
        z_pos = lax.broadcasted_iota(jnp.int32, (depth_z, reach), 0).astype(jnp.float32)
        zc, zs = cos_sin(uz * z_pos)
        y_pos = lax.broadcasted_iota(jnp.int32, (TY, reach), 0).astype(jnp.float32)
        yc, ys = cos_sin(uy * y_pos)
        for ty in range(TY):
            c, s = yc[ty : ty + 1, :], ys[ty : ty + 1, :]
            block = pl.ds(ty * depth_z, depth_z)
            table[m, block, pl.ds(0, reach)] = (zc * c - zs * s).astype(jnp.bfloat16)
            table[m, block, pl.ds(reach, reach)] = (zc * s + zs * c).astype(jnp.bfloat16)
        return carry

    phases = 2 * STEPS
    share = -(-owners // phases)

    def build_share(phase):
        lax.fori_loop(
            jnp.minimum(phase * share, owners), jnp.minimum((phase + 1) * share, owners), build, 0
        )

    lane2 = lax.broadcasted_iota(jnp.int32, (width_y, LANES), 1)
    row2 = lax.broadcasted_iota(jnp.int32, (width_y, LANES), 0)

    def face_copies(step, kind, ghosts, toward):
        result = []
        for axis, ((name, index, count), ghost, source) in enumerate(
            zip(place_in, ghosts, (sx, sy, sz))
        ):
            copy = pltpu.make_async_remote_copy(
                src_ref=source.at[kind, step],
                dst_ref=ghost.at[step],
                send_sem=face_send.at[kind, axis],
                recv_sem=face_recv.at[step, kind, axis],
                device_id={name: index + toward},
                device_id_type=MESH,
            )
            low, high = index > 0, index < count - 1
            result.append((low, high, copy) if toward < 0 else (high, low, copy))
        return result

    def start_all(copies):
        for sends, _, copy in copies:
            pl.when(sends)(copy.start)

    def wait_all(copies):
        for sends, receives, copy in copies:
            pl.when(sends)(copy.wait_send)
            pl.when(receives)(copy.wait_recv)

    def pack_z(pairs, from_lane):
        total = jnp.zeros((width_y, LANES), jnp.float32)
        for k, plane in enumerate(pairs):
            for x in range(width_x):
                at = k * width_x + x
                rolled = pltpu.roll(plane(x), (at - from_lane) % LANES, 1)
                total = jnp.where(lane2 == at, rolled, total)
        return total

    def step_body(step, carry):
        now, old = lax.rem(step, 2), lax.rem(step + 1, 2)
        sx[0, step, 0] = ele[1, 0]
        sx[0, step, 1] = ele[2, 0]
        sy[0, step, 0] = ele[0, pl.ds(0, width_x), 0, :]
        sy[0, step, 1] = ele[2, pl.ds(0, width_x), 0, :]
        sz[0, step] = pack_z((lambda x: ele[0, x], lambda x: ele[1, x]), 0)
        copies = face_copies(step, 0, (e_x, e_y, e_z), -1)
        start_all(copies)
        build_share(2 * step)
        wait_all(copies)
        ele[1, width_x] = e_x[step, 0]
        ele[2, width_x] = e_x[step, 1]
        packed = e_z[step]
        for x in range(width_x):
            ex, ey, ez = ele[0, x], ele[1, x], ele[2, x]

            def up_y(f, k):
                return jnp.where(
                    row2 == width_y - 1, e_y[step, k, x : x + 1, :], pltpu.roll(f, width_y - 1, 0)
                )

            def up_z(f, k):
                ghost = pltpu.roll(packed, (LANES - 1 - k * width_x - x) % LANES, 1)
                return jnp.where(lane2 == LANES - 1, ghost, pltpu.roll(f, LANES - 1, 1))

            hx = mag[0, x + 1] - SPEED * ((up_y(ez, 1) - ez) - (up_z(ey, 1) - ey))
            hy = mag[1, x + 1] - SPEED * ((up_z(ex, 0) - ex) - (ele[2, x + 1] - ez))
            hz = mag[2, x + 1] - SPEED * ((ele[1, x + 1] - ey) - (up_y(ex, 0) - ex))
            mag[0, x + 1] = hx
            mag[1, x + 1] = hy
            mag[2, x + 1] = hz
        sx[1, step, 0] = mag[1, width_x]
        sx[1, step, 1] = mag[2, width_x]
        sy[1, step, 0] = mag[0, pl.ds(1, width_x), width_y - 1, :]
        sy[1, step, 1] = mag[2, pl.ds(1, width_x), width_y - 1, :]
        sz[1, step] = pack_z((lambda x: mag[0, x + 1], lambda x: mag[1, x + 1]), depth_z - 1)
        copies = face_copies(step, 1, (h_x, h_y, h_z), 1)
        start_all(copies)
        build_share(2 * step + 1)
        wait_all(copies)
        mag[1, 0] = h_x[step, 0]
        mag[2, 0] = h_x[step, 1]
        packed_h = h_z[step]
        angle = [WAVE * SPEED * (n + 0.5) for n in range(STEPS)]
        angle_e = [WAVE * SPEED * (n + 1.0) for n in range(STEPS)]
        cos_h, sin_h = pick(step, [math.cos(a) for a in angle]), pick(step, [math.sin(a) for a in angle])
        cos_e, sin_e = pick(step, [math.cos(a) for a in angle_e]), pick(step, [math.sin(a) for a in angle_e])
        for x in range(width_x):
            hx, hy, hz = mag[0, x + 1], mag[1, x + 1], mag[2, x + 1]

            def down_y(f, k):
                return jnp.where(row2 == 0, h_y[step, k, x : x + 1, :], pltpu.roll(f, 1, 0))

            def down_z(f, k):
                ghost = pltpu.roll(packed_h, (-k * width_x - x) % LANES, 1)
                return jnp.where(lane2 == 0, ghost, pltpu.roll(f, 1, 1))

            curl = (
                (hz - down_y(hz, 1)) - (hy - down_z(hy, 1)),
                (hx - down_z(hx, 0)) - (hz - mag[2, x]),
                (hy - mag[1, x]) - (hx - down_y(hx, 0)),
            )
            e = [ele[c, x] for c in range(3)]
            sat = 1.0 / (1.0 + e[0] * e[0] + e[1] * e[1] + e[2] * e[2])
            a, b, strength, sheet = coef[0, x], coef[1, x], coef[2, x] * sat, coef[3, x]
            for c in range(3):
                p = pq[now, c, x]
                pn = a * p + b * pq[old, c, x] + strength * e[c]
                pq[old, c, x] = pn
                e[c] = e[c] + SPEED * curl[c] - sheet * (pn - p)
                ele[c, x] = e[c]
            terms = (
                -cos_h * hz, sin_h * hz, cos_h * hy, -sin_h * hy,
                cos_e * e[2], -sin_e * e[2], -cos_e * e[1], sin_e * e[1],
            )
            for c, term in enumerate(terms):
                for k in range(blocks_y):
                    at = x * blocks_y + k
                    acc[c, at] = acc[c, at] + term[k * TY : (k + 1) * TY]
        return carry

    acc[...] = jnp.zeros_like(acc)
    lax.fori_loop(0, STEPS, step_body, 0)
    for c in range(3):
        out_ref[c] = ele[c, pl.ds(0, width_x)]
        out_ref[3 + c] = mag[c, pl.ds(1, width_x)]

    for j in range(0, slots, 2):
        p, q = place_ref[0, iz, j], place_ref[0, iz, min(j + 1, slots - 1)]
        for ty in range(TY):
            pair = jnp.concatenate([acc[:, p, ty, :], acc[:, q, ty, :]], axis=0)
            cur[0, pl.ds(j * 8, 16), pl.ds(ty * depth_z, depth_z)] = pair.astype(jnp.bfloat16)

    partner = {"gy": iy + 1 - 2 * parity}
    to_pair = [
        pltpu.make_async_remote_copy(
            src_ref=buffer.at[0], dst_ref=buffer.at[1],
            send_sem=pair_send.at[k], recv_sem=pair_recv.at[k],
            device_id=partner, device_id_type=MESH,
        )
        for k, buffer in enumerate((cur, coords))
    ]
    for copy in to_pair:
        copy.start()
    for copy in to_pair:
        copy.wait()

    scale = 1.0 / math.sqrt(n_x * n_y * n_z * TILE_MEAN * TY * depth_z)
    even = lax.rem(lax.broadcasted_iota(jnp.int32, (8, reach), 0), 2) == 0

    def far_copy(o):
        m = lax.rem(me + o, owners)
        return pltpu.make_async_remote_copy(
            src_ref=blocks.at[o], dst_ref=landed.at[o],
            send_sem=far_send.at[o], recv_sem=far_recv.at[o],
            device_id=owner_device(m), device_id_type=MESH,
        )

    def far_block(o):
        m = lax.rem(me + o, owners)
        ux, uy, uz = dirs[m, 0:1, :], dirs[m, 1:2, :], dirs[m, 2:3, :]
        u = jnp.zeros((8, reach), jnp.float32)
        v = jnp.zeros((8, reach), jnp.float32)
        for half in range(2):
            at = coords[half]
            tc, ts = cos_sin(at[:, 0:1] * ux + at[:, 1:2] * uy + at[:, 2:3] * uz)
            tc, ts = tc * at[:, 3:4], ts * at[:, 3:4]
            product = jnp.dot(cur[half], table[m], preferred_element_type=jnp.float32)
            for j in range(slots):
                pc = product[j * 8 : j * 8 + 8, :reach]
                ps = product[j * 8 : j * 8 + 8, reach:]
                c, s = tc[j : j + 1, :], ts[j : j + 1, :]
                u = u + (pc * c - ps * s)
                v = v + (pc * s + ps * c)
        blocks[o] = jnp.where(even, u - pltpu.roll(v, 7, 0), u + pltpu.roll(v, 1, 0)) * scale

    def far_step(o, carry):
        far_block(o)
        far_copy(o).start()
        return carry

    lax.fori_loop(1, owners, far_step, 0)
    far_block(0)

    def gather_step(o, total):
        far_copy(o).wait()
        return total + landed[o]

    total = lax.fori_loop(1, owners, gather_step, blocks[0])
    far_ref[...] = total


def shards(
    fields, polarization, material, omega0, damping, strength,
    tile_count, tile_place, dir_angles, dir_order,
):
    sizes = tuple(lax.axis_size(name) for name in ("gx", "gy", "gz"))
    n_x, n_y, n_z = sizes
    devices = n_x * n_y * n_z
    width_x, width_y, depth_z = material.shape
    slots = tile_place.shape[2]
    count = dir_order.shape[0]
    reach = count // devices
    owners = devices // 2
    angles = dir_angles.reshape(2, count // LANES, LANES).transpose(0, 2, 1)
    angles = angles.reshape(2 * LANES, count // LANES)
    order = dir_order.reshape(n_x * (n_y // 2), 2, n_z, 1, reach)
    even_slots = slots + slots % 2
    coord_rows = -(-slots // 8) * 8
    f32 = jnp.float32
    vmem, smem = pl.BlockSpec(memory_space=pltpu.VMEM), pl.BlockSpec(memory_space=pltpu.SMEM)
    x_face, y_face, z_face = (2, width_y, depth_z), (2, width_x, depth_z), (width_y, LANES)
    fields_out, far = pl.pallas_call(
        functools.partial(kernel, sizes, slots, 2 * reach),
        out_shape=(
            jax.ShapeDtypeStruct(fields.shape, f32),
            jax.ShapeDtypeStruct((8, reach), f32),
        ),
        in_specs=[vmem] * 3 + [smem] * 5 + [vmem] * 2,
        out_specs=(vmem, vmem),
        scratch_shapes=[
            pltpu.VMEM((3, width_x + 1, width_y, depth_z), f32),
            pltpu.VMEM((3, width_x + 1, width_y, depth_z), f32),
            pltpu.VMEM((2, 3, width_x, width_y, depth_z), f32),
            pltpu.VMEM((4, width_x, width_y, depth_z), f32),
            pltpu.VMEM((8, width_x * width_y // TY, TY, depth_z), f32),
            pltpu.VMEM((2, even_slots * 8, TY * depth_z), jnp.bfloat16),
            pltpu.VMEM((2, coord_rows, LANES), f32),
            pltpu.VMEM((owners, 8, reach), f32),
            pltpu.VMEM((owners, TY * depth_z, 2 * reach), jnp.bfloat16),
            pltpu.VMEM((owners, 8, reach), f32),
            pltpu.VMEM((owners, 8, reach), f32),
        ]
        + [pltpu.VMEM((STEPS,) + face, f32) for face in (x_face, y_face, z_face)] * 2
        + [pltpu.VMEM((2, STEPS) + face, f32) for face in (x_face, y_face, z_face)]
        + [
            pltpu.SemaphoreType.DMA((2, 3)),
            pltpu.SemaphoreType.DMA((STEPS, 2, 3)),
            pltpu.SemaphoreType.DMA((2,)),
            pltpu.SemaphoreType.DMA((2,)),
            pltpu.SemaphoreType.DMA((owners,)),
            pltpu.SemaphoreType.DMA((owners,)),
        ],
        compiler_params=pltpu.CompilerParams(
            collective_id=0, has_side_effects=True, vmem_limit_bytes=56 * 1024 * 1024
        ),
    )(
        fields, polarization, material, omega0, damping, strength,
        tile_count, tile_place, angles, order,
    )
    return fields_out, far.T


def solution(mesh):
    placed = (
        P(None, "gx", "gy", "gz"),
        P(None, "gx", "gy", "gz"),
        P("gx", "gy", "gz"),
        P(),
        P(),
        P(),
        P(("gx", "gy"), None),
        P(("gx", "gy"), None, None),
        P(),
        P(),
    )
    return jax.shard_map(
        shards,
        mesh=mesh,
        in_specs=placed,
        out_specs=(P(None, "gx", "gy", "gz"), P(("gx", "gy", "gz"), None)),
        check_vma=False,
    )
```

```python
import functools
import math

import jax
import jax.numpy as jnp
from jax import lax
from jax.experimental import pallas as pl
from jax.experimental.pallas import tpu as pltpu
from jax.sharding import PartitionSpec as P

TY = 8
STEPS = 4
TILE_MEAN = 6
SPEED = 0.5
WAVE = 0.35
LANES = 128
MESH = pl.DeviceIdType.MESH

SIN_TERMS = (
    6.283185302511505, -41.34170040531808, 81.60513138582216, -76.70301535428969,
    42.02592698929055, -14.899846680245616, 3.238137526404064,
)
COS_TERMS = (
    0.9999999890590243, -19.73920449945407, 64.93911745990263, -85.45013953100009,
    60.16763095180868, -25.967599251355935, 6.528658164931359,
)


def poly(s, terms):
    total = jnp.full_like(s, terms[-1])
    for term in terms[-2::-1]:
        total = total * s + term
    return total


def cos_sin(turns):
    t = turns - jnp.round(turns)
    s = t * t
    return poly(s, COS_TERMS), t * poly(s, SIN_TERMS)


def pick(step, values):
    result = jnp.float32(values[-1])
    for index in range(len(values) - 2, -1, -1):
        result = jnp.where(step == index, jnp.float32(values[index]), result)
    return result


def kernel(
    sizes, slots, reach,
    fields_ref, pol_ref, mat_ref, omega_ref, damp_ref, strength_ref, count_ref, place_ref,
    angles_ref, order_ref,
    out_ref, far_ref,
    ele, mag, pq, coef, acc, folded, coords, spread, parts, dirs, table, blocks, landed,
    e_x, e_y, e_z, h_x, h_y, h_z, sx, sy, sz,
    face_send, face_recv, pair_send, pair_recv, far_send, far_recv,
):
    n_x, n_y, n_z = sizes
    half_y = n_y // 2
    owners = n_x * half_y * n_z
    width_x, width_y, depth_z = mat_ref.shape
    blocks_y = width_y // TY
    ix, iy, iz = lax.axis_index("gx"), lax.axis_index("gy"), lax.axis_index("gz")
    parity = lax.rem(iy, 2)
    me = (ix * half_y + iy // 2) * n_z + iz
    place_in = (("gx", ix, n_x), ("gy", iy, n_y), ("gz", iz, n_z))

    def owner_device(m):
        return {
            "gx": m // (half_y * n_z),
            "gy": lax.rem(m // n_z, half_y) * 2 + parity,
            "gz": lax.rem(m, n_z),
        }

    for ghost in (e_x, e_y, e_z, h_x, h_y, h_z):
        ghost[...] = jnp.zeros_like(ghost)

    barrier = pltpu.get_barrier_semaphore()

    def greet(o, carry):
        pl.semaphore_signal(
            barrier, inc=1, device_id=owner_device(lax.rem(me + o, owners)), device_id_type=MESH
        )
        return carry

    lax.fori_loop(1, owners, greet, 0)

    @pl.when(iy > 0)
    def _():
        pl.semaphore_signal(barrier, inc=1, device_id={"gy": iy - 1}, device_id_type=MESH)

    @pl.when(iy < n_y - 1)
    def _():
        pl.semaphore_signal(barrier, inc=1, device_id={"gy": iy + 1}, device_id_type=MESH)

    for c in range(3):
        ele[c, pl.ds(0, width_x)] = fields_ref[c]
        mag[c, pl.ds(1, width_x)] = fields_ref[3 + c]
        pq[0, c] = pol_ref[c]
        pq[1, c] = pol_ref[3 + c]
    material = mat_ref[...]
    coefs = [jnp.zeros(material.shape, jnp.float32) for _ in range(3)]
    for m in range(omega_ref.shape[0]):
        w, g, s = omega_ref[m], damp_ref[m], strength_ref[m]
        w, g, s = (jnp.full((1, 1, depth_z), v, jnp.float32) for v in (w, g, s))
        below = 1.0 + 0.5 * g
        chosen = material == m + 1
        for i, v in enumerate(((2.0 - w * w) / below, -(1.0 - 0.5 * g) / below, s * (w * w) / below)):
            coefs[i] = jnp.where(chosen, v, coefs[i])
    for i in range(3):
        coef[i] = coefs[i]
    coef[3] = jnp.where(material > 0, 1.0, 0.0).astype(jnp.float32)

    first_x, first_y, first_z = ix * width_x, iy * width_y, iz * depth_z
    lane = lax.broadcasted_iota(jnp.int32, (1, LANES), 1)
    coords[0] = jnp.zeros(coords.shape[1:], jnp.float32)
    for j in range(slots):
        p = place_ref[0, iz, j]
        x0 = (first_x + p // blocks_y).astype(jnp.float32)
        y0 = (first_y + lax.rem(p, blocks_y) * TY).astype(jnp.float32)
        z0 = first_z.astype(jnp.float32) + 0.5 * (depth_z - 1)
        live = jnp.where(j < count_ref[0, iz], jnp.float32(1.0), jnp.float32(0.0))
        row = jnp.where(lane == 0, x0, 0.0) + jnp.where(lane == 1, y0 + 0.5 * (TY - 1), 0.0)
        row = row + jnp.where(lane == 2, z0, 0.0) + jnp.where(lane == 3, live, 0.0)
        coords[0, j : j + 1, :] = row

    high_count = spread.shape[1]
    for a in range(2):
        for h in range(high_count):
            spread[a, h : h + 1, :] = angles_ref[a : a + 1, h * LANES : (h + 1) * LANES]
        whole = spread[a]
        part_a = whole.astype(jnp.bfloat16).astype(jnp.float32)
        part_b = (whole - part_a).astype(jnp.bfloat16).astype(jnp.float32)
        part_c = whole - part_a - part_b
        parts[a] = jnp.concatenate([part_a, part_b, part_c], axis=0).T.astype(jnp.bfloat16)

    pl.semaphore_wait(
        barrier,
        owners - 1 + jnp.where(iy > 0, 1, 0) + jnp.where(iy < n_y - 1, 1, 0),
    )

    half_z = depth_z // 2
    per_turn = WAVE / (2.0 * math.pi)

    def build(m, carry):
        chosen = order_ref[m // n_z, parity, lax.rem(m, n_z)]
        high = lax.rem(lax.broadcasted_iota(jnp.int32, (3 * high_count, reach), 0), high_count)
        low = lax.broadcasted_iota(jnp.int32, (LANES, reach), 0)
        hot = jnp.where(high == chosen // LANES, 1.0, 0.0).astype(jnp.bfloat16)
        own = low == lax.rem(chosen, LANES)
        theta, phi = (
            jnp.sum(
                jnp.where(own, jnp.dot(parts[a], hot, preferred_element_type=jnp.float32), 0.0),
                axis=0,
                keepdims=True,
            )
            for a in range(2)
        )
        ct, st = cos_sin(theta * (1.0 / (2.0 * math.pi)))
        cp, sp = cos_sin(phi * (1.0 / (2.0 * math.pi)))
        ux, uy, uz = st * cp * per_turn, st * sp * per_turn, ct * per_turn
        dirs[m, 0:1, :] = ux
        dirs[m, 1:2, :] = uy
        dirs[m, 2:3, :] = uz
        z_pos = lax.broadcasted_iota(jnp.int32, (half_z, reach), 0).astype(jnp.float32) + 0.5
        zc, zs = cos_sin(uz * z_pos)
        y_pos = lax.broadcasted_iota(jnp.int32, (8, reach), 0).astype(jnp.float32) + 0.5
        yc, ys = cos_sin(uy * y_pos)
        for k in range(TY // 2):
            c, s = yc[k : k + 1, :], ys[k : k + 1, :]
            upper, lower = pl.ds(k * depth_z, half_z), pl.ds(k * depth_z + half_z, half_z)
            table[m, 0, upper, :] = (zc * c).astype(jnp.bfloat16)
            table[m, 0, lower, :] = (zs * -s).astype(jnp.bfloat16)
            table[m, 1, upper, :] = (zc * s).astype(jnp.bfloat16)
            table[m, 1, lower, :] = (zs * c).astype(jnp.bfloat16)
        return carry

    phases = 2 * STEPS
    share = -(-owners // phases)

    def build_share(phase):
        lax.fori_loop(
            jnp.minimum(phase * share, owners), jnp.minimum((phase + 1) * share, owners), build, 0
        )

    lane2 = lax.broadcasted_iota(jnp.int32, (width_y, LANES), 1)
    row2 = lax.broadcasted_iota(jnp.int32, (width_y, LANES), 0)

    def face_copies(step, kind, ghosts, toward):
        result = []
        for axis, ((name, index, count), ghost, source) in enumerate(
            zip(place_in, ghosts, (sx, sy, sz))
        ):
            copy = pltpu.make_async_remote_copy(
                src_ref=source.at[kind, step],
                dst_ref=ghost.at[step],
                send_sem=face_send.at[kind, axis],
                recv_sem=face_recv.at[step, kind, axis],
                device_id={name: index + toward},
                device_id_type=MESH,
            )
            low, high = index > 0, index < count - 1
            result.append((low, high, copy) if toward < 0 else (high, low, copy))
        return result

    def start_all(copies):
        for sends, _, copy in copies:
            pl.when(sends)(copy.start)

    def wait_all(copies):
        for sends, receives, copy in copies:
            pl.when(sends)(copy.wait_send)
            pl.when(receives)(copy.wait_recv)

    def pack_z(pairs, from_lane):
        total = jnp.zeros((width_y, LANES), jnp.float32)
        for k, plane in enumerate(pairs):
            for x in range(width_x):
                at = k * width_x + x
                rolled = pltpu.roll(plane(x), (at - from_lane) % LANES, 1)
                total = jnp.where(lane2 == at, rolled, total)
        return total

    def add_phasors(x, first, terms):
        for c, term in enumerate(terms):
            for k in range(blocks_y):
                at = x * blocks_y + k
                acc[first + c, at] = acc[first + c, at] + term[k * TY : (k + 1) * TY]

    def add_electric(cos_e, sin_e):
        for x in range(width_x):
            ey, ez = ele[1, x], ele[2, x]
            add_phasors(x, 4, (cos_e * ez, -sin_e * ez, -cos_e * ey, sin_e * ey))

    angle_h = [WAVE * SPEED * (n + 0.5) for n in range(STEPS)]
    angle_e = [WAVE * SPEED * (n + 1.0) for n in range(STEPS)]

    def step_body(step, carry):
        now, old = lax.rem(step, 2), lax.rem(step + 1, 2)
        sx[0, step, 0] = ele[1, 0]
        sx[0, step, 1] = ele[2, 0]
        sy[0, step, 0] = ele[0, pl.ds(0, width_x), 0, :]
        sy[0, step, 1] = ele[2, pl.ds(0, width_x), 0, :]
        sz[0, step] = pack_z((lambda x: ele[0, x], lambda x: ele[1, x]), 0)
        copies = face_copies(step, 0, (e_x, e_y, e_z), -1)
        start_all(copies)
        build_share(2 * step)
        add_electric(
            pick(step, [0.0] + [math.cos(a) for a in angle_e[:-1]]),
            pick(step, [0.0] + [math.sin(a) for a in angle_e[:-1]]),
        )
        wait_all(copies)
        ele[1, width_x] = e_x[step, 0]
        ele[2, width_x] = e_x[step, 1]
        packed = e_z[step]
        for x in range(width_x):
            ex, ey, ez = ele[0, x], ele[1, x], ele[2, x]

            def up_y(f, k):
                return jnp.where(
                    row2 == width_y - 1, e_y[step, k, x : x + 1, :], pltpu.roll(f, width_y - 1, 0)
                )

            def up_z(f, k):
                ghost = pltpu.roll(packed, (LANES - 1 - k * width_x - x) % LANES, 1)
                return jnp.where(lane2 == LANES - 1, ghost, pltpu.roll(f, LANES - 1, 1))

            hx = mag[0, x + 1] - SPEED * ((up_y(ez, 1) - ez) - (up_z(ey, 1) - ey))
            hy = mag[1, x + 1] - SPEED * ((up_z(ex, 0) - ex) - (ele[2, x + 1] - ez))
            hz = mag[2, x + 1] - SPEED * ((ele[1, x + 1] - ey) - (up_y(ex, 0) - ex))
            mag[0, x + 1] = hx
            mag[1, x + 1] = hy
            mag[2, x + 1] = hz
        sx[1, step, 0] = mag[1, width_x]
        sx[1, step, 1] = mag[2, width_x]
        sy[1, step, 0] = mag[0, pl.ds(1, width_x), width_y - 1, :]
        sy[1, step, 1] = mag[2, pl.ds(1, width_x), width_y - 1, :]
        sz[1, step] = pack_z((lambda x: mag[0, x + 1], lambda x: mag[1, x + 1]), depth_z - 1)
        copies = face_copies(step, 1, (h_x, h_y, h_z), 1)
        start_all(copies)
        build_share(2 * step + 1)
        cos_h = pick(step, [math.cos(a) for a in angle_h])
        sin_h = pick(step, [math.sin(a) for a in angle_h])
        for x in range(width_x):
            e = [ele[c, x] for c in range(3)]
            sat = 1.0 / (1.0 + e[0] * e[0] + e[1] * e[1] + e[2] * e[2])
            a, b, strength, sheet = coef[0, x], coef[1, x], coef[2, x] * sat, coef[3, x]
            for c in range(3):
                p = pq[now, c, x]
                pn = a * p + b * pq[old, c, x] + strength * e[c]
                pq[old, c, x] = pn
                ele[c, x] = e[c] - sheet * (pn - p)
            hy, hz = mag[1, x + 1], mag[2, x + 1]
            add_phasors(x, 0, (-cos_h * hz, sin_h * hz, cos_h * hy, -sin_h * hy))
        wait_all(copies)
        mag[1, 0] = h_x[step, 0]
        mag[2, 0] = h_x[step, 1]
        packed_h = h_z[step]
        for x in range(width_x):
            hx, hy, hz = mag[0, x + 1], mag[1, x + 1], mag[2, x + 1]

            def down_y(f, k):
                return jnp.where(row2 == 0, h_y[step, k, x : x + 1, :], pltpu.roll(f, 1, 0))

            def down_z(f, k):
                ghost = pltpu.roll(packed_h, (-k * width_x - x) % LANES, 1)
                return jnp.where(lane2 == 0, ghost, pltpu.roll(f, 1, 1))

            curl = (
                (hz - down_y(hz, 1)) - (hy - down_z(hy, 1)),
                (hx - down_z(hx, 0)) - (hz - mag[2, x]),
                (hy - mag[1, x]) - (hx - down_y(hx, 0)),
            )
            for c in range(3):
                ele[c, x] = ele[c, x] + SPEED * curl[c]
        return carry

    acc[...] = jnp.zeros_like(acc)
    lax.fori_loop(0, STEPS, step_body, 0)
    add_electric(math.cos(angle_e[-1]), math.sin(angle_e[-1]))

    row_z = lax.broadcasted_iota(jnp.int32, (depth_z, depth_z), 0)
    col_z = lax.broadcasted_iota(jnp.int32, (depth_z, depth_z), 1)
    offset = lax.rem(col_z, half_z)
    mirror = jnp.where(col_z < half_z, 1.0, -1.0)
    fold = jnp.where(row_z == half_z + offset, 1.0, 0.0)
    fold = (fold + jnp.where(row_z == half_z - 1 - offset, mirror, 0.0)).astype(jnp.bfloat16)
    height = folded.shape[1] // 2
    places = [place_ref[0, iz, min(j, slots - 1)] for j in range(height // 8)]
    split = []
    for ty in range(TY):
        rows_ty = jnp.concatenate([acc[:, p, ty, :] for p in places], axis=0).astype(jnp.bfloat16)
        split.append(jnp.dot(rows_ty, fold, preferred_element_type=jnp.float32))
    first_half = lax.broadcasted_iota(jnp.int32, (height, depth_z), 1) < half_z
    for k in range(TY // 2):
        above, under = split[TY // 2 + k], split[TY // 2 - 1 - k]
        same, other = above + under, above - under
        block = pl.ds(k * depth_z, depth_z)
        folded[0, pl.ds(0, height), block] = jnp.where(first_half, same, other).astype(jnp.bfloat16)
        folded[1, pl.ds(0, height), block] = jnp.where(first_half, other, same).astype(jnp.bfloat16)

    partner = {"gy": iy + 1 - 2 * parity}
    to_pair = [
        pltpu.make_async_remote_copy(
            src_ref=source, dst_ref=target,
            send_sem=pair_send.at[k], recv_sem=pair_recv.at[k],
            device_id=partner, device_id_type=MESH,
        )
        for k, (source, target) in enumerate((
            (folded.at[0, pl.ds(0, height)], folded.at[0, pl.ds(height, height)]),
            (folded.at[1, pl.ds(0, height)], folded.at[1, pl.ds(height, height)]),
            (coords.at[0], coords.at[1]),
        ))
    ]
    for copy in to_pair:
        copy.start()
    for c in range(3):
        out_ref[c] = ele[c, pl.ds(0, width_x)]
        out_ref[3 + c] = mag[c, pl.ds(1, width_x)]

    scale = 1.0 / math.sqrt(n_x * n_y * n_z * TILE_MEAN * TY * depth_z)
    even = lax.rem(lax.broadcasted_iota(jnp.int32, (8, reach), 0), 2) == 0

    def far_copy(o):
        m = lax.rem(me + o, owners)
        return pltpu.make_async_remote_copy(
            src_ref=blocks.at[o], dst_ref=landed.at[o],
            send_sem=far_send.at[o], recv_sem=far_recv.at[o],
            device_id=owner_device(m), device_id_type=MESH,
        )

    def add_tiles(sums, m, first, halves):
        u, v = sums
        ux, uy, uz = dirs[m, 0:1, :], dirs[m, 1:2, :], dirs[m, 2:3, :]
        part = pl.ds(first * height, halves * height)
        in_cos = jnp.dot(folded[0, part], table[m, 0], preferred_element_type=jnp.float32)
        in_sin = jnp.dot(folded[1, part], table[m, 1], preferred_element_type=jnp.float32)
        for half in range(halves):
            at = coords[first + half]
            tc, ts = cos_sin(at[:, 0:1] * ux + at[:, 1:2] * uy + at[:, 2:3] * uz)
            tc, ts = tc * at[:, 3:4], ts * at[:, 3:4]
            for j in range(slots):
                row = half * height + j * 8
                pc, ps = in_cos[row : row + 8], in_sin[row : row + 8]
                c, s = tc[j : j + 1, :], ts[j : j + 1, :]
                u = u + (pc * c - ps * s)
                v = v + (pc * s + ps * c)
        return u, v

    empty = (jnp.zeros((8, reach), jnp.float32), jnp.zeros((8, reach), jnp.float32))

    def keep_block(o, sums):
        u, v = sums
        blocks[o] = jnp.where(even, u - pltpu.roll(v, 7, 0), u + pltpu.roll(v, 1, 0)) * scale

    def far_step(o, carry):
        keep_block(o, add_tiles(empty, lax.rem(me + o, owners), 0, 2))
        far_copy(o).start()
        return carry

    sums = add_tiles(empty, me, 0, 1)
    for copy in to_pair:
        copy.wait()
    lax.fori_loop(1, owners, far_step, 0)
    keep_block(0, add_tiles(sums, me, 1, 1))

    def gather_step(o, total):
        far_copy(o).wait()
        return total + landed[o]

    total = lax.fori_loop(1, owners, gather_step, blocks[0])
    far_ref[...] = total


def shards(
    fields, polarization, material, omega0, damping, strength,
    tile_count, tile_place, dir_angles, dir_order,
):
    sizes = tuple(lax.axis_size(name) for name in ("gx", "gy", "gz"))
    n_x, n_y, n_z = sizes
    devices = n_x * n_y * n_z
    width_x, width_y, depth_z = material.shape
    slots = tile_place.shape[2]
    count = dir_order.shape[0]
    reach = count // devices
    owners = devices // 2
    order = dir_order.reshape(n_x * (n_y // 2), 2, n_z, 1, reach)
    even_slots = slots + slots % 2
    coord_rows = -(-slots // 8) * 8
    f32 = jnp.float32
    vmem, smem = pl.BlockSpec(memory_space=pltpu.VMEM), pl.BlockSpec(memory_space=pltpu.SMEM)
    x_face, y_face, z_face = (2, width_y, depth_z), (2, width_x, depth_z), (width_y, LANES)
    fields_out, far = pl.pallas_call(
        functools.partial(kernel, sizes, slots, reach),
        out_shape=(
            jax.ShapeDtypeStruct(fields.shape, f32),
            jax.ShapeDtypeStruct((8, reach), f32),
        ),
        in_specs=[vmem] * 3 + [smem] * 5 + [vmem] * 2,
        out_specs=(vmem, vmem),
        scratch_shapes=[
            pltpu.VMEM((3, width_x + 1, width_y, depth_z), f32),
            pltpu.VMEM((3, width_x + 1, width_y, depth_z), f32),
            pltpu.VMEM((2, 3, width_x, width_y, depth_z), f32),
            pltpu.VMEM((4, width_x, width_y, depth_z), f32),
            pltpu.VMEM((8, width_x * width_y // TY, TY, depth_z), f32),
            pltpu.VMEM((2, 2 * even_slots * 8, TY // 2 * depth_z), jnp.bfloat16),
            pltpu.VMEM((2, coord_rows, LANES), f32),
            pltpu.VMEM((2, count // LANES, LANES), f32),
            pltpu.VMEM((2, LANES, 3 * (count // LANES)), jnp.bfloat16),
            pltpu.VMEM((owners, 8, reach), f32),
            pltpu.VMEM((owners, 2, TY // 2 * depth_z, reach), jnp.bfloat16),
            pltpu.VMEM((owners, 8, reach), f32),
            pltpu.VMEM((owners, 8, reach), f32),
        ]
        + [pltpu.VMEM((STEPS,) + face, f32) for face in (x_face, y_face, z_face)] * 2
        + [pltpu.VMEM((2, STEPS) + face, f32) for face in (x_face, y_face, z_face)]
        + [
            pltpu.SemaphoreType.DMA((2, 3)),
            pltpu.SemaphoreType.DMA((STEPS, 2, 3)),
            pltpu.SemaphoreType.DMA((3,)),
            pltpu.SemaphoreType.DMA((3,)),
            pltpu.SemaphoreType.DMA((owners,)),
            pltpu.SemaphoreType.DMA((owners,)),
        ],
        compiler_params=pltpu.CompilerParams(
            collective_id=0, has_side_effects=True, vmem_limit_bytes=56 * 1024 * 1024
        ),
    )(
        fields, polarization, material, omega0, damping, strength,
        tile_count, tile_place, dir_angles, order,
    )
    return fields_out, far.T


def solution(mesh):
    placed = (
        P(None, "gx", "gy", "gz"),
        P(None, "gx", "gy", "gz"),
        P("gx", "gy", "gz"),
        P(),
        P(),
        P(),
        P(("gx", "gy"), None),
        P(("gx", "gy"), None, None),
        P(),
        P(),
    )
    return jax.shard_map(
        shards,
        mesh=mesh,
        in_specs=placed,
        out_specs=(P(None, "gx", "gy", "gz"), P(("gx", "gy", "gz"), None)),
        check_vma=False,
    )
```

```python
import functools
import math

import jax
import jax.numpy as jnp
from jax import lax
from jax.experimental import pallas as pl
from jax.experimental.pallas import tpu as pltpu
from jax.sharding import PartitionSpec as P

TY = 8
STEPS = 4
TILE_MEAN = 6
SPEED = 0.5
WAVE = 0.35
LANES = 128
MESH = pl.DeviceIdType.MESH

SIN_TERMS = (
    6.283185302511505, -41.34170040531808, 81.60513138582216, -76.70301535428969,
    42.02592698929055, -14.899846680245616, 3.238137526404064,
)
COS_TERMS = (
    0.9999999890590243, -19.73920449945407, 64.93911745990263, -85.45013953100009,
    60.16763095180868, -25.967599251355935, 6.528658164931359,
)


def poly(s, terms):
    total = jnp.full_like(s, terms[-1])
    for term in terms[-2::-1]:
        total = total * s + term
    return total


def cos_sin(turns):
    t = turns - jnp.round(turns)
    s = t * t
    return poly(s, COS_TERMS), t * poly(s, SIN_TERMS)


def pick(step, values):
    result = jnp.float32(values[-1])
    for index in range(len(values) - 2, -1, -1):
        result = jnp.where(step == index, jnp.float32(values[index]), result)
    return result


def kernel(
    sizes, slots, reach,
    fields_ref, pol_ref, mat_ref, omega_ref, damp_ref, strength_ref, count_ref, place_ref,
    angles_ref, order_ref,
    out_ref, far_ref,
    ele, mag, pq, coef, acc, folded, coords, spread, parts, dirs, table, blocks, landed,
    e_x, e_y, e_z, h_x, h_y, h_z, edge, sx, sy, sz, edge_out,
    face_send, face_recv, pair_send, pair_recv, far_send, far_recv,
):
    n_x, n_y, n_z = sizes
    half_y = n_y // 2
    owners = n_x * half_y * n_z
    width_x, width_y, depth_z = mat_ref.shape
    blocks_y = width_y // TY
    ix, iy, iz = lax.axis_index("gx"), lax.axis_index("gy"), lax.axis_index("gz")
    parity = lax.rem(iy, 2)
    me = (ix * half_y + iy // 2) * n_z + iz
    place_in = (("gx", ix, n_x), ("gy", iy, n_y), ("gz", iz, n_z))

    def owner_device(m):
        return {
            "gx": m // (half_y * n_z),
            "gy": lax.rem(m // n_z, half_y) * 2 + parity,
            "gz": lax.rem(m, n_z),
        }

    for ghost in (e_x, e_y, e_z, h_x, h_y, h_z, edge, edge_out):
        ghost[...] = jnp.zeros_like(ghost)

    barrier = pltpu.get_barrier_semaphore()

    def greet(o, carry):
        pl.semaphore_signal(
            barrier, inc=1, device_id=owner_device(lax.rem(me + o, owners)), device_id_type=MESH
        )
        return carry

    lax.fori_loop(1, owners, greet, 0)

    def exists(offset):
        found = jnp.int32(1)
        for (_, index, count), move in zip(place_in, offset):
            if move:
                found = found * jnp.where((index + move >= 0) & (index + move < count), 1, 0)
        return found

    def device_at(offset):
        return {name: index + move for (name, index, _), move in zip(place_in, offset) if move}

    others = ((0, 1, 0), (0, -1, 0), (1, -1, 0), (-1, 1, 0), (0, 1, -1), (0, -1, 1))
    for offset in others:
        pl.when(exists(offset) > 0)(
            functools.partial(
                pl.semaphore_signal,
                barrier, inc=1, device_id=device_at(offset), device_id_type=MESH,
            )
        )

    for c in range(3):
        ele[c, pl.ds(0, width_x)] = fields_ref[c]
        mag[c, pl.ds(1, width_x)] = fields_ref[3 + c]
        pq[0, c] = pol_ref[c]
        pq[1, c] = pol_ref[3 + c]
    material = mat_ref[...]
    coefs = [jnp.zeros(material.shape, jnp.float32) for _ in range(3)]
    for m in range(omega_ref.shape[0]):
        w, g, s = omega_ref[m], damp_ref[m], strength_ref[m]
        w, g, s = (jnp.full((1, 1, depth_z), v, jnp.float32) for v in (w, g, s))
        below = 1.0 + 0.5 * g
        chosen = material == m + 1
        for i, v in enumerate(((2.0 - w * w) / below, -(1.0 - 0.5 * g) / below, s * (w * w) / below)):
            coefs[i] = jnp.where(chosen, v, coefs[i])
    for i in range(3):
        coef[i] = coefs[i]
    coef[3] = jnp.where(material > 0, 1.0, 0.0).astype(jnp.float32)

    first_x, first_y, first_z = ix * width_x, iy * width_y, iz * depth_z
    lane = lax.broadcasted_iota(jnp.int32, (1, LANES), 1)
    coords[0] = jnp.zeros(coords.shape[1:], jnp.float32)
    for j in range(slots):
        p = place_ref[0, iz, j]
        x0 = (first_x + p // blocks_y).astype(jnp.float32)
        y0 = (first_y + lax.rem(p, blocks_y) * TY).astype(jnp.float32)
        z0 = first_z.astype(jnp.float32) + 0.5 * (depth_z - 1)
        live = jnp.where(j < count_ref[0, iz], jnp.float32(1.0), jnp.float32(0.0))
        row = jnp.where(lane == 0, x0, 0.0) + jnp.where(lane == 1, y0 + 0.5 * (TY - 1), 0.0)
        row = row + jnp.where(lane == 2, z0, 0.0) + jnp.where(lane == 3, live, 0.0)
        coords[0, j : j + 1, :] = row

    high_count = spread.shape[1]
    for a in range(2):
        for h in range(high_count):
            spread[a, h : h + 1, :] = angles_ref[a : a + 1, h * LANES : (h + 1) * LANES]
        whole = spread[a]
        part_a = whole.astype(jnp.bfloat16).astype(jnp.float32)
        part_b = (whole - part_a).astype(jnp.bfloat16).astype(jnp.float32)
        part_c = whole - part_a - part_b
        parts[a] = jnp.concatenate([part_a, part_b, part_c], axis=0).T.astype(jnp.bfloat16)

    pl.semaphore_wait(
        barrier,
        owners - 1 + sum(exists(offset) for offset in others),
    )

    half_z = depth_z // 2
    per_turn = WAVE / (2.0 * math.pi)

    def build(m, carry):
        chosen = order_ref[m // n_z, parity, lax.rem(m, n_z)]
        high = lax.rem(lax.broadcasted_iota(jnp.int32, (3 * high_count, reach), 0), high_count)
        low = lax.broadcasted_iota(jnp.int32, (LANES, reach), 0)
        hot = jnp.where(high == chosen // LANES, 1.0, 0.0).astype(jnp.bfloat16)
        own = low == lax.rem(chosen, LANES)
        theta, phi = (
            jnp.sum(
                jnp.where(own, jnp.dot(parts[a], hot, preferred_element_type=jnp.float32), 0.0),
                axis=0,
                keepdims=True,
            )
            for a in range(2)
        )
        ct, st = cos_sin(theta * (1.0 / (2.0 * math.pi)))
        cp, sp = cos_sin(phi * (1.0 / (2.0 * math.pi)))
        ux, uy, uz = st * cp * per_turn, st * sp * per_turn, ct * per_turn
        dirs[m, 0:1, :] = ux
        dirs[m, 1:2, :] = uy
        dirs[m, 2:3, :] = uz
        z_pos = lax.broadcasted_iota(jnp.int32, (half_z, reach), 0).astype(jnp.float32) + 0.5
        zc, zs = cos_sin(uz * z_pos)
        y_pos = lax.broadcasted_iota(jnp.int32, (8, reach), 0).astype(jnp.float32) + 0.5
        yc, ys = cos_sin(uy * y_pos)
        for k in range(TY // 2):
            c, s = yc[k : k + 1, :], ys[k : k + 1, :]
            upper, lower = pl.ds(k * depth_z, half_z), pl.ds(k * depth_z + half_z, half_z)
            table[m, 0, upper, :] = (zc * c).astype(jnp.bfloat16)
            table[m, 0, lower, :] = (zs * -s).astype(jnp.bfloat16)
            table[m, 1, upper, :] = (zc * s).astype(jnp.bfloat16)
            table[m, 1, lower, :] = (zs * c).astype(jnp.bfloat16)
        return carry

    phases = STEPS
    share = -(-owners // phases)

    def build_share(phase):
        lax.fori_loop(
            jnp.minimum(phase * share, owners), jnp.minimum((phase + 1) * share, owners), build, 0
        )

    lane2 = lax.broadcasted_iota(jnp.int32, (width_y, LANES), 1)
    row2 = lax.broadcasted_iota(jnp.int32, (width_y, LANES), 0)
    lane3 = lax.broadcasted_iota(jnp.int32, (width_x, LANES), 1)
    row3 = lax.broadcasted_iota(jnp.int32, (width_x, LANES), 0)

    def copies_of(step, group):
        low = ((-1, 0, 0), (0, -1, 0), (0, 0, -1))
        high = ((1, 0, 0), (0, 1, 0), (0, 0, 1))
        across = ((1, 0, -1), (1, -1, 0), (0, 1, -1), (-1, 1, 0), (0, -1, 1), (-1, 0, 1))
        if group == 0:
            ends = [(s.at[0, step], d.at[step]) for s, d in zip((sx, sy, sz), (e_x, e_y, e_z))]
            moves = list(zip(low, ends))
            ends = [(edge_out.at[step, k], edge.at[step, k]) for k in range(6)]
            moves = moves + list(zip(across, ends))
        else:
            ends = [(s.at[1, step], d.at[step]) for s, d in zip((sx, sy, sz), (h_x, h_y, h_z))]
            moves = list(zip(high, ends))
        result = []
        for k, (offset, (source, target)) in enumerate(moves):
            copy = pltpu.make_async_remote_copy(
                src_ref=source,
                dst_ref=target,
                send_sem=face_send.at[group * 9 + k],
                recv_sem=face_recv.at[step, group * 9 + k],
                device_id=device_at(offset),
                device_id_type=MESH,
            )
            result.append((exists(offset) > 0, exists(tuple(-m for m in offset)) > 0, copy))
        return result

    def start_all(copies):
        for sends, _, copy in copies:
            pl.when(sends)(copy.start)

    def wait_all(copies):
        for sends, receives, copy in copies:
            pl.when(sends)(copy.wait_send)
            pl.when(receives)(copy.wait_recv)

    def pack_z(pairs, from_lane):
        total = jnp.zeros((width_y, LANES), jnp.float32)
        for k, plane in enumerate(pairs):
            for x in range(width_x):
                at = k * width_x + x
                rolled = pltpu.roll(plane(x), (at - from_lane) % LANES, 1)
                total = jnp.where(lane2 == at, rolled, total)
        return total

    def add_phasors(x, first, terms):
        for c, term in enumerate(terms):
            for k in range(blocks_y):
                at = x * blocks_y + k
                acc[first + c, at] = acc[first + c, at] + term[k * TY : (k + 1) * TY]

    def add_electric(cos_e, sin_e):
        for x in range(width_x):
            ey, ez = ele[1, x], ele[2, x]
            add_phasors(x, 4, (cos_e * ez, -sin_e * ez, -cos_e * ey, sin_e * ey))

    angle_h = [WAVE * SPEED * (n + 0.5) for n in range(STEPS)]
    angle_e = [WAVE * SPEED * (n + 1.0) for n in range(STEPS)]

    def step_body(step, carry):
        now, old = lax.rem(step, 2), lax.rem(step + 1, 2)
        sx[0, step, 0] = ele[1, 0]
        sx[0, step, 1] = ele[2, 0]
        sy[0, step, 0] = ele[0, pl.ds(0, width_x), 0, :]
        sy[0, step, 1] = ele[2, pl.ds(0, width_x), 0, :]
        sz[0, step] = pack_z((lambda x: ele[0, x], lambda x: ele[1, x]), 0)
        last_x, last_y, last_z = width_x - 1, width_y - 1, depth_z - 1
        edge_out[step, 0, pl.ds(0, width_y)] = pltpu.roll(ele[0, last_x], last_z, 1)
        edge_out[step, 1, 0:1] = ele[0, last_x, 0:1, :]
        edge_out[step, 2, pl.ds(0, width_x)] = pltpu.roll(ele[1, pl.ds(0, width_x), last_y, :], last_z, 1)
        edge_out[step, 3, 0:1] = ele[1, 0, last_y : last_y + 1, :]
        edge_out[step, 4, 0:1] = pack_z((lambda x: ele[2, x],), last_z)[0:1]
        at = 2 * width_x - 1
        edge_out[step, 5, pl.ds(0, width_y)] = pltpu.roll(ele[2, 0], (at - last_z) % LANES, 1)
        electric_copies = copies_of(step, 0)
        start_all(electric_copies)

        for x in range(width_x):
            ex, ey, ez = ele[0, x], ele[1, x], ele[2, x]

            def up_y(f):
                return jnp.where(row2 == last_y, 0.0, pltpu.roll(f, last_y, 0))

            def up_z(f):
                return jnp.where(lane2 == last_z, 0.0, pltpu.roll(f, last_z, 1))

            ahead_y = ele[1, x + 1] if x < last_x else jnp.zeros_like(ey)
            ahead_z = ele[2, x + 1] if x < last_x else jnp.zeros_like(ez)
            mag[0, x + 1] = mag[0, x + 1] - SPEED * ((up_y(ez) - ez) - (up_z(ey) - ey))
            mag[1, x + 1] = mag[1, x + 1] - SPEED * ((up_z(ex) - ex) - (ahead_z - ez))
            mag[2, x + 1] = mag[2, x + 1] - SPEED * ((ahead_y - ey) - (up_y(ex) - ex))
        sx[1, step, 0] = mag[1, width_x]
        sx[1, step, 1] = mag[2, width_x]
        sy[1, step, 0] = mag[0, pl.ds(1, width_x), last_y, :]
        sy[1, step, 1] = mag[2, pl.ds(1, width_x), last_y, :]
        sz[1, step] = pack_z((lambda x: mag[0, x + 1], lambda x: mag[1, x + 1]), last_z)
        magnetic_copies = copies_of(step, 1)
        start_all(magnetic_copies)

        build_share(step)
        add_electric(
            pick(step, [0.0] + [math.cos(a) for a in angle_e[:-1]]),
            pick(step, [0.0] + [math.sin(a) for a in angle_e[:-1]]),
        )
        for x in range(width_x):
            e = [ele[c, x] for c in range(3)]
            sat = 1.0 / (1.0 + e[0] * e[0] + e[1] * e[1] + e[2] * e[2])
            a, b, strength, sheet = coef[0, x], coef[1, x], coef[2, x] * sat, coef[3, x]
            for c in range(3):
                p = pq[now, c, x]
                pn = a * p + b * pq[old, c, x] + strength * e[c]
                pq[old, c, x] = pn
                ele[c, x] = e[c] - sheet * (pn - p)
        wait_all(electric_copies)
        wait_all(magnetic_copies)

        in_x, in_y, in_z = (
            jnp.where(index > 0, jnp.float32(SPEED), jnp.float32(0.0)) for _, index, _ in place_in
        )
        edges = [edge[step, k] for k in range(6)]

        def only(condition, value):
            return jnp.where(condition, value, 0.0)

        mag[1, 0] = h_x[step, 0] + in_x * (
            sx[0, step, 1] - only(lane2 == last_z, edges[0][:width_y])
        )
        mag[2, 0] = h_x[step, 1] - in_x * (sx[0, step, 0] - only(row2 == last_y, edges[1][0:1]))
        below_y = (
            h_y[step, 0] - in_y * (sy[0, step, 1] - only(lane3 == last_z, edges[2][:width_x])),
            h_y[step, 1] + in_y * (sy[0, step, 0] - only(row3 == last_x, edges[3][0:1])),
        )
        own = sz[0, step]
        for_x = only(lane2 < width_x, pltpu.roll(own, LANES - width_x, 1))
        for_x = for_x - only((row2 == last_y) & (lane2 < width_x), edges[4][0:1])
        for_y = only((lane2 >= width_x) & (lane2 < 2 * width_x), pltpu.roll(own, width_x, 1))
        for_y = for_y - only(lane2 == at, edges[5][:width_y])
        below_z = h_z[step] + in_z * (for_x - for_y)
        above_z = e_z[step]

        cos_h = pick(step, [math.cos(a) for a in angle_h])
        sin_h = pick(step, [math.sin(a) for a in angle_h])
        for x in range(width_x):
            def beyond_y(k):
                return only(row2 == last_y, SPEED * e_y[step, k, x : x + 1, :])

            def beyond_z(k):
                ghost = pltpu.roll(above_z, (LANES - 1 - k * width_x - x) % LANES, 1)
                return only(lane2 == last_z, SPEED * ghost)

            hx = mag[0, x + 1] - beyond_y(1) + beyond_z(1)
            hy = mag[1, x + 1] - beyond_z(0)
            hz = mag[2, x + 1] + beyond_y(0)
            if x == last_x:
                hy = hy + SPEED * e_x[step, 1]
                hz = hz - SPEED * e_x[step, 0]
            mag[0, x + 1] = hx
            mag[1, x + 1] = hy
            mag[2, x + 1] = hz

            def down_y(f, k):
                return jnp.where(row2 == 0, below_y[k][x : x + 1, :], pltpu.roll(f, 1, 0))

            def down_z(f, k):
                ghost = pltpu.roll(below_z, (-k * width_x - x) % LANES, 1)
                return jnp.where(lane2 == 0, ghost, pltpu.roll(f, 1, 1))

            curl = (
                (hz - down_y(hz, 1)) - (hy - down_z(hy, 1)),
                (hx - down_z(hx, 0)) - (hz - mag[2, x]),
                (hy - mag[1, x]) - (hx - down_y(hx, 0)),
            )
            for c in range(3):
                ele[c, x] = ele[c, x] + SPEED * curl[c]
            add_phasors(x, 0, (-cos_h * hz, sin_h * hz, cos_h * hy, -sin_h * hy))
        return carry

    acc[...] = jnp.zeros_like(acc)
    lax.fori_loop(0, STEPS, step_body, 0)
    add_electric(math.cos(angle_e[-1]), math.sin(angle_e[-1]))

    row_z = lax.broadcasted_iota(jnp.int32, (depth_z, depth_z), 0)
    col_z = lax.broadcasted_iota(jnp.int32, (depth_z, depth_z), 1)
    offset = lax.rem(col_z, half_z)
    mirror = jnp.where(col_z < half_z, 1.0, -1.0)
    fold = jnp.where(row_z == half_z + offset, 1.0, 0.0)
    fold = (fold + jnp.where(row_z == half_z - 1 - offset, mirror, 0.0)).astype(jnp.bfloat16)
    height = folded.shape[1] // 2
    places = [place_ref[0, iz, min(j, slots - 1)] for j in range(height // 8)]
    split = []
    for ty in range(TY):
        rows_ty = jnp.concatenate([acc[:, p, ty, :] for p in places], axis=0).astype(jnp.bfloat16)
        split.append(jnp.dot(rows_ty, fold, preferred_element_type=jnp.float32))
    first_half = lax.broadcasted_iota(jnp.int32, (height, depth_z), 1) < half_z
    for k in range(TY // 2):
        above, under = split[TY // 2 + k], split[TY // 2 - 1 - k]
        same, other = above + under, above - under
        block = pl.ds(k * depth_z, depth_z)
        folded[0, pl.ds(0, height), block] = jnp.where(first_half, same, other).astype(jnp.bfloat16)
        folded[1, pl.ds(0, height), block] = jnp.where(first_half, other, same).astype(jnp.bfloat16)

    partner = {"gy": iy + 1 - 2 * parity}
    to_pair = [
        pltpu.make_async_remote_copy(
            src_ref=source, dst_ref=target,
            send_sem=pair_send.at[k], recv_sem=pair_recv.at[k],
            device_id=partner, device_id_type=MESH,
        )
        for k, (source, target) in enumerate((
            (folded.at[0, pl.ds(0, height)], folded.at[0, pl.ds(height, height)]),
            (folded.at[1, pl.ds(0, height)], folded.at[1, pl.ds(height, height)]),
            (coords.at[0], coords.at[1]),
        ))
    ]
    for copy in to_pair:
        copy.start()
    for c in range(3):
        out_ref[c] = ele[c, pl.ds(0, width_x)]
        out_ref[3 + c] = mag[c, pl.ds(1, width_x)]

    scale = 1.0 / math.sqrt(n_x * n_y * n_z * TILE_MEAN * TY * depth_z)
    even = lax.rem(lax.broadcasted_iota(jnp.int32, (8, reach), 0), 2) == 0

    def far_copy(o):
        m = lax.rem(me + o, owners)
        return pltpu.make_async_remote_copy(
            src_ref=blocks.at[o], dst_ref=landed.at[o],
            send_sem=far_send.at[o], recv_sem=far_recv.at[o],
            device_id=owner_device(m), device_id_type=MESH,
        )

    def add_tiles(sums, m, first, halves):
        u, v = sums
        ux, uy, uz = dirs[m, 0:1, :], dirs[m, 1:2, :], dirs[m, 2:3, :]
        part = pl.ds(first * height, halves * height)
        in_cos = jnp.dot(folded[0, part], table[m, 0], preferred_element_type=jnp.float32)
        in_sin = jnp.dot(folded[1, part], table[m, 1], preferred_element_type=jnp.float32)
        for half in range(halves):
            at = coords[first + half]
            tc, ts = cos_sin(at[:, 0:1] * ux + at[:, 1:2] * uy + at[:, 2:3] * uz)
            tc, ts = tc * at[:, 3:4], ts * at[:, 3:4]
            for j in range(slots):
                row = half * height + j * 8
                pc, ps = in_cos[row : row + 8], in_sin[row : row + 8]
                c, s = tc[j : j + 1, :], ts[j : j + 1, :]
                u = u + (pc * c - ps * s)
                v = v + (pc * s + ps * c)
        return u, v

    empty = (jnp.zeros((8, reach), jnp.float32), jnp.zeros((8, reach), jnp.float32))

    def keep_block(o, sums):
        u, v = sums
        blocks[o] = jnp.where(even, u - pltpu.roll(v, 7, 0), u + pltpu.roll(v, 1, 0)) * scale

    def far_step(o, carry):
        keep_block(o, add_tiles(empty, lax.rem(me + o, owners), 0, 2))
        far_copy(o).start()
        return carry

    sums = add_tiles(empty, me, 0, 1)
    for copy in to_pair:
        copy.wait()
    lax.fori_loop(1, owners, far_step, 0)
    keep_block(0, add_tiles(sums, me, 1, 1))

    def gather_step(o, total):
        far_copy(o).wait()
        return total + landed[o]

    total = lax.fori_loop(1, owners, gather_step, blocks[0])
    far_ref[...] = total


def shards(
    fields, polarization, material, omega0, damping, strength,
    tile_count, tile_place, dir_angles, dir_order,
):
    sizes = tuple(lax.axis_size(name) for name in ("gx", "gy", "gz"))
    n_x, n_y, n_z = sizes
    devices = n_x * n_y * n_z
    width_x, width_y, depth_z = material.shape
    slots = tile_place.shape[2]
    count = dir_order.shape[0]
    reach = count // devices
    owners = devices // 2
    order = dir_order.reshape(n_x * (n_y // 2), 2, n_z, 1, reach)
    even_slots = slots + slots % 2
    coord_rows = -(-slots // 8) * 8
    f32 = jnp.float32
    vmem, smem = pl.BlockSpec(memory_space=pltpu.VMEM), pl.BlockSpec(memory_space=pltpu.SMEM)
    x_face, y_face, z_face = (2, width_y, depth_z), (2, width_x, depth_z), (width_y, LANES)
    fields_out, far = pl.pallas_call(
        functools.partial(kernel, sizes, slots, reach),
        out_shape=(
            jax.ShapeDtypeStruct(fields.shape, f32),
            jax.ShapeDtypeStruct((8, reach), f32),
        ),
        in_specs=[vmem] * 3 + [smem] * 5 + [vmem] * 2,
        out_specs=(vmem, vmem),
        scratch_shapes=[
            pltpu.VMEM((3, width_x + 1, width_y, depth_z), f32),
            pltpu.VMEM((3, width_x + 1, width_y, depth_z), f32),
            pltpu.VMEM((2, 3, width_x, width_y, depth_z), f32),
            pltpu.VMEM((4, width_x, width_y, depth_z), f32),
            pltpu.VMEM((8, width_x * width_y // TY, TY, depth_z), f32),
            pltpu.VMEM((2, 2 * even_slots * 8, TY // 2 * depth_z), jnp.bfloat16),
            pltpu.VMEM((2, coord_rows, LANES), f32),
            pltpu.VMEM((2, count // LANES, LANES), f32),
            pltpu.VMEM((2, LANES, 3 * (count // LANES)), jnp.bfloat16),
            pltpu.VMEM((owners, 8, reach), f32),
            pltpu.VMEM((owners, 2, TY // 2 * depth_z, reach), jnp.bfloat16),
            pltpu.VMEM((owners, 8, reach), f32),
            pltpu.VMEM((owners, 8, reach), f32),
        ]
        + [pltpu.VMEM((STEPS,) + face, f32) for face in (x_face, y_face, z_face)] * 2
        + [pltpu.VMEM((STEPS, 6, max(width_x, width_y), LANES), f32)]
        + [pltpu.VMEM((2, STEPS) + face, f32) for face in (x_face, y_face, z_face)]
        + [pltpu.VMEM((STEPS, 6, max(width_x, width_y), LANES), f32)]
        + [
            pltpu.SemaphoreType.DMA((12,)),
            pltpu.SemaphoreType.DMA((STEPS, 12)),
            pltpu.SemaphoreType.DMA((3,)),
            pltpu.SemaphoreType.DMA((3,)),
            pltpu.SemaphoreType.DMA((owners,)),
            pltpu.SemaphoreType.DMA((owners,)),
        ],
        compiler_params=pltpu.CompilerParams(
            collective_id=0, has_side_effects=True, vmem_limit_bytes=56 * 1024 * 1024
        ),
    )(
        fields, polarization, material, omega0, damping, strength,
        tile_count, tile_place, dir_angles, order,
    )
    return fields_out, far.T


def solution(mesh):
    placed = (
        P(None, "gx", "gy", "gz"),
        P(None, "gx", "gy", "gz"),
        P("gx", "gy", "gz"),
        P(),
        P(),
        P(),
        P(("gx", "gy"), None),
        P(("gx", "gy"), None, None),
        P(),
        P(),
    )
    return jax.shard_map(
        shards,
        mesh=mesh,
        in_specs=placed,
        out_specs=(P(None, "gx", "gy", "gz"), P(("gx", "gy", "gz"), None)),
        check_vma=False,
    )
```

```python
import functools
import math

import jax
import jax.numpy as jnp
from jax import lax
from jax.experimental import pallas as pl
from jax.experimental.pallas import tpu as pltpu
from jax.sharding import PartitionSpec as P

TY = 8
STEPS = 4
TILE_MEAN = 6
SPEED = 0.5
WAVE = 0.35
LANES = 128
MESH = pl.DeviceIdType.MESH

SIN_TERMS = (
    6.283185302511505, -41.34170040531808, 81.60513138582216, -76.70301535428969,
    42.02592698929055, -14.899846680245616, 3.238137526404064,
)
COS_TERMS = (
    0.9999999890590243, -19.73920449945407, 64.93911745990263, -85.45013953100009,
    60.16763095180868, -25.967599251355935, 6.528658164931359,
)


def poly(s, terms):
    total = jnp.full_like(s, terms[-1])
    for term in terms[-2::-1]:
        total = total * s + term
    return total


def cos_sin(turns):
    t = turns - jnp.round(turns)
    s = t * t
    return poly(s, COS_TERMS), t * poly(s, SIN_TERMS)


def pick(step, values):
    result = jnp.float32(values[-1])
    for index in range(len(values) - 2, -1, -1):
        result = jnp.where(step == index, jnp.float32(values[index]), result)
    return result


def kernel(
    sizes, slots, reach,
    fields_ref, pol_ref, mat_ref, omega_ref, damp_ref, strength_ref, count_ref, place_ref,
    angles_ref, order_ref,
    out_ref, far_ref,
    ele, mag, pq, coef, acc, folded, coords, spread, parts, dirs, table, blocks, landed,
    e_x, e_y, e_z, h_x, h_y, h_z, edge, sx, sy, sz, edge_out,
    face_send, face_recv, pair_send, pair_recv, far_send, far_recv, in_sem, out_sem,
):
    n_x, n_y, n_z = sizes
    half_y = n_y // 2
    owners = n_x * half_y * n_z
    width_x, width_y, depth_z = mat_ref.shape
    blocks_y = width_y // TY
    ix, iy, iz = lax.axis_index("gx"), lax.axis_index("gy"), lax.axis_index("gz")
    parity = lax.rem(iy, 2)
    me = (ix * half_y + iy // 2) * n_z + iz
    place_in = (("gx", ix, n_x), ("gy", iy, n_y), ("gz", iz, n_z))

    def owner_device(m):
        return {
            "gx": m // (half_y * n_z),
            "gy": lax.rem(m // n_z, half_y) * 2 + parity,
            "gz": lax.rem(m, n_z),
        }

    loads = []
    for c in range(3):
        loads.append((fields_ref.at[c], ele.at[c, pl.ds(0, width_x)]))
        loads.append((fields_ref.at[3 + c], mag.at[c, pl.ds(1, width_x)]))
        loads.append((pol_ref.at[c], pq.at[0, c]))
        loads.append((pol_ref.at[3 + c], pq.at[1, c]))
    loads = [pltpu.make_async_copy(a, b, in_sem.at[k]) for k, (a, b) in enumerate(loads)]
    for copy in loads:
        copy.start()

    for ghost in (e_x, e_y, e_z, h_x, h_y, h_z, edge, edge_out):
        ghost[...] = jnp.zeros_like(ghost)

    barrier = pltpu.get_barrier_semaphore()

    def greet(o, carry):
        pl.semaphore_signal(
            barrier, inc=1, device_id=owner_device(lax.rem(me + o, owners)), device_id_type=MESH
        )
        return carry

    lax.fori_loop(1, owners, greet, 0)

    def exists(offset):
        found = jnp.int32(1)
        for (_, index, count), move in zip(place_in, offset):
            if move:
                found = found * jnp.where((index + move >= 0) & (index + move < count), 1, 0)
        return found

    def device_at(offset):
        return {name: index + move for (name, index, _), move in zip(place_in, offset) if move}

    others = ((0, 1, 0), (0, -1, 0), (1, -1, 0), (-1, 1, 0), (0, 1, -1), (0, -1, 1))
    for offset in others:
        pl.when(exists(offset) > 0)(
            functools.partial(
                pl.semaphore_signal,
                barrier, inc=1, device_id=device_at(offset), device_id_type=MESH,
            )
        )

    material = mat_ref[...]
    coefs = [jnp.zeros(material.shape, jnp.float32) for _ in range(3)]
    for m in range(omega_ref.shape[0]):
        w, g, s = omega_ref[m], damp_ref[m], strength_ref[m]
        w, g, s = (jnp.full((1, 1, depth_z), v, jnp.float32) for v in (w, g, s))
        below = 1.0 + 0.5 * g
        chosen = material == m + 1
        for i, v in enumerate(((2.0 - w * w) / below, -(1.0 - 0.5 * g) / below, s * (w * w) / below)):
            coefs[i] = jnp.where(chosen, v, coefs[i])
    for i in range(3):
        coef[i] = coefs[i]
    coef[3] = jnp.where(material > 0, 1.0, 0.0).astype(jnp.float32)

    first_x, first_y, first_z = ix * width_x, iy * width_y, iz * depth_z
    lane = lax.broadcasted_iota(jnp.int32, (1, LANES), 1)
    coords[0] = jnp.zeros(coords.shape[1:], jnp.float32)
    for j in range(slots):
        p = place_ref[0, iz, j]
        x0 = (first_x + p // blocks_y).astype(jnp.float32)
        y0 = (first_y + lax.rem(p, blocks_y) * TY).astype(jnp.float32)
        z0 = first_z.astype(jnp.float32) + 0.5 * (depth_z - 1)
        live = jnp.where(j < count_ref[0, iz], jnp.float32(1.0), jnp.float32(0.0))
        row = jnp.where(lane == 0, x0, 0.0) + jnp.where(lane == 1, y0 + 0.5 * (TY - 1), 0.0)
        row = row + jnp.where(lane == 2, z0, 0.0) + jnp.where(lane == 3, live, 0.0)
        coords[0, j : j + 1, :] = row

    high_count = spread.shape[1]
    for a in range(2):
        for h in range(high_count):
            spread[a, h : h + 1, :] = angles_ref[a : a + 1, h * LANES : (h + 1) * LANES]
        whole = spread[a]
        part_a = whole.astype(jnp.bfloat16).astype(jnp.float32)
        part_b = (whole - part_a).astype(jnp.bfloat16).astype(jnp.float32)
        part_c = whole - part_a - part_b
        parts[a] = jnp.concatenate([part_a, part_b, part_c], axis=0).T.astype(jnp.bfloat16)

    pl.semaphore_wait(
        barrier,
        owners - 1 + sum(exists(offset) for offset in others),
    )

    half_z = depth_z // 2
    per_turn = WAVE / (2.0 * math.pi)

    def build(m, carry):
        chosen = order_ref[m // n_z, parity, lax.rem(m, n_z)]
        high = lax.rem(lax.broadcasted_iota(jnp.int32, (3 * high_count, reach), 0), high_count)
        low = lax.broadcasted_iota(jnp.int32, (LANES, reach), 0)
        hot = jnp.where(high == chosen // LANES, 1.0, 0.0).astype(jnp.bfloat16)
        own = low == lax.rem(chosen, LANES)
        theta, phi = (
            jnp.sum(
                jnp.where(own, jnp.dot(parts[a], hot, preferred_element_type=jnp.float32), 0.0),
                axis=0,
                keepdims=True,
            )
            for a in range(2)
        )
        ct, st = cos_sin(theta * (1.0 / (2.0 * math.pi)))
        cp, sp = cos_sin(phi * (1.0 / (2.0 * math.pi)))
        ux, uy, uz = st * cp * per_turn, st * sp * per_turn, ct * per_turn
        dirs[m, 0:1, :] = ux
        dirs[m, 1:2, :] = uy
        dirs[m, 2:3, :] = uz
        z_pos = lax.broadcasted_iota(jnp.int32, (half_z, reach), 0).astype(jnp.float32) + 0.5
        zc, zs = cos_sin(uz * z_pos)
        y_pos = lax.broadcasted_iota(jnp.int32, (8, reach), 0).astype(jnp.float32) + 0.5
        yc, ys = cos_sin(uy * y_pos)
        for k in range(TY // 2):
            c, s = yc[k : k + 1, :], ys[k : k + 1, :]
            upper, lower = pl.ds(k * depth_z, half_z), pl.ds(k * depth_z + half_z, half_z)
            table[m, 0, upper, :] = (zc * c).astype(jnp.bfloat16)
            table[m, 0, lower, :] = (zs * -s).astype(jnp.bfloat16)
            table[m, 1, upper, :] = (zc * s).astype(jnp.bfloat16)
            table[m, 1, lower, :] = (zs * c).astype(jnp.bfloat16)
        return carry

    phases = STEPS
    share = -(-owners // phases)
    group = math.gcd(owners // phases, 4) if owners % phases == 0 else 1

    def build_share(phase):
        first = jnp.minimum(phase * share, owners)
        count = jnp.minimum(share, owners - first) // group

        def build_group(i, carry):
            for r in range(group):
                build(first + i * group + r, carry)
            return carry

        lax.fori_loop(0, count, build_group, 0)

    lane2 = lax.broadcasted_iota(jnp.int32, (width_y, LANES), 1)
    row2 = lax.broadcasted_iota(jnp.int32, (width_y, LANES), 0)
    lane3 = lax.broadcasted_iota(jnp.int32, (width_x, LANES), 1)
    row3 = lax.broadcasted_iota(jnp.int32, (width_x, LANES), 0)

    def copies_of(step, group):
        low = ((-1, 0, 0), (0, -1, 0), (0, 0, -1))
        high = ((1, 0, 0), (0, 1, 0), (0, 0, 1))
        across = ((1, 0, -1), (1, -1, 0), (0, 1, -1), (-1, 1, 0), (0, -1, 1), (-1, 0, 1))
        if group == 0:
            ends = [(s.at[0, step], d.at[step]) for s, d in zip((sx, sy, sz), (e_x, e_y, e_z))]
            moves = list(zip(low, ends))
            ends = [(edge_out.at[step, k], edge.at[step, k]) for k in range(6)]
            moves = moves + list(zip(across, ends))
        else:
            ends = [(s.at[1, step], d.at[step]) for s, d in zip((sx, sy, sz), (h_x, h_y, h_z))]
            moves = list(zip(high, ends))
        result = []
        for k, (offset, (source, target)) in enumerate(moves):
            copy = pltpu.make_async_remote_copy(
                src_ref=source,
                dst_ref=target,
                send_sem=face_send.at[group * 9 + k],
                recv_sem=face_recv.at[step, group * 9 + k],
                device_id=device_at(offset),
                device_id_type=MESH,
            )
            result.append((exists(offset) > 0, exists(tuple(-m for m in offset)) > 0, copy))
        return result

    def start_all(copies):
        for sends, _, copy in copies:
            pl.when(sends)(copy.start)

    def wait_all(copies):
        for sends, receives, copy in copies:
            pl.when(sends)(copy.wait_send)
            pl.when(receives)(copy.wait_recv)

    def pack_z(pairs, from_lane):
        total = jnp.zeros((width_y, LANES), jnp.float32)
        for k, plane in enumerate(pairs):
            for x in range(width_x):
                at = k * width_x + x
                rolled = pltpu.roll(plane(x), (at - from_lane) % LANES, 1)
                total = jnp.where(lane2 == at, rolled, total)
        return total

    def add_phasors(x, first, terms):
        for c, term in enumerate(terms):
            for k in range(blocks_y):
                at = x * blocks_y + k
                acc[first + c, at] = acc[first + c, at] + term[k * TY : (k + 1) * TY]

    def add_electric(cos_e, sin_e):
        for x in range(width_x):
            ey, ez = ele[1, x], ele[2, x]
            add_phasors(x, 4, (cos_e * ez, -sin_e * ez, -cos_e * ey, sin_e * ey))

    angle_h = [WAVE * SPEED * (n + 0.5) for n in range(STEPS)]
    angle_e = [WAVE * SPEED * (n + 1.0) for n in range(STEPS)]

    def step_body(step, carry):
        now, old = lax.rem(step, 2), lax.rem(step + 1, 2)
        sx[0, step, 0] = ele[1, 0]
        sx[0, step, 1] = ele[2, 0]
        sy[0, step, 0] = ele[0, pl.ds(0, width_x), 0, :]
        sy[0, step, 1] = ele[2, pl.ds(0, width_x), 0, :]
        sz[0, step] = pack_z((lambda x: ele[0, x], lambda x: ele[1, x]), 0)
        last_x, last_y, last_z = width_x - 1, width_y - 1, depth_z - 1
        edge_out[step, 0, pl.ds(0, width_y)] = pltpu.roll(ele[0, last_x], last_z, 1)
        edge_out[step, 1, 0:1] = ele[0, last_x, 0:1, :]
        edge_out[step, 2, pl.ds(0, width_x)] = pltpu.roll(ele[1, pl.ds(0, width_x), last_y, :], last_z, 1)
        edge_out[step, 3, 0:1] = ele[1, 0, last_y : last_y + 1, :]
        edge_out[step, 4, 0:1] = pack_z((lambda x: ele[2, x],), last_z)[0:1]
        at = 2 * width_x - 1
        edge_out[step, 5, pl.ds(0, width_y)] = pltpu.roll(ele[2, 0], (at - last_z) % LANES, 1)
        electric_copies = copies_of(step, 0)
        start_all(electric_copies)

        for x in range(width_x):
            ex, ey, ez = ele[0, x], ele[1, x], ele[2, x]

            def up_y(f):
                return jnp.where(row2 == last_y, 0.0, pltpu.roll(f, last_y, 0))

            def up_z(f):
                return jnp.where(lane2 == last_z, 0.0, pltpu.roll(f, last_z, 1))

            ahead_y = ele[1, x + 1] if x < last_x else jnp.zeros_like(ey)
            ahead_z = ele[2, x + 1] if x < last_x else jnp.zeros_like(ez)
            mag[0, x + 1] = mag[0, x + 1] - SPEED * ((up_y(ez) - ez) - (up_z(ey) - ey))
            mag[1, x + 1] = mag[1, x + 1] - SPEED * ((up_z(ex) - ex) - (ahead_z - ez))
            mag[2, x + 1] = mag[2, x + 1] - SPEED * ((ahead_y - ey) - (up_y(ex) - ex))
        sx[1, step, 0] = mag[1, width_x]
        sx[1, step, 1] = mag[2, width_x]
        sy[1, step, 0] = mag[0, pl.ds(1, width_x), last_y, :]
        sy[1, step, 1] = mag[2, pl.ds(1, width_x), last_y, :]
        sz[1, step] = pack_z((lambda x: mag[0, x + 1], lambda x: mag[1, x + 1]), last_z)
        magnetic_copies = copies_of(step, 1)
        start_all(magnetic_copies)

        build_share(step)
        add_electric(
            pick(step, [0.0] + [math.cos(a) for a in angle_e[:-1]]),
            pick(step, [0.0] + [math.sin(a) for a in angle_e[:-1]]),
        )
        for x in range(width_x):
            e = [ele[c, x] for c in range(3)]
            sat = 1.0 / (1.0 + e[0] * e[0] + e[1] * e[1] + e[2] * e[2])
            a, b, strength, sheet = coef[0, x], coef[1, x], coef[2, x] * sat, coef[3, x]
            for c in range(3):
                p = pq[now, c, x]
                pn = a * p + b * pq[old, c, x] + strength * e[c]
                pq[old, c, x] = pn
                ele[c, x] = e[c] - sheet * (pn - p)
        wait_all(electric_copies)
        wait_all(magnetic_copies)

        in_x, in_y, in_z = (
            jnp.where(index > 0, jnp.float32(SPEED), jnp.float32(0.0)) for _, index, _ in place_in
        )
        edges = [edge[step, k] for k in range(6)]

        def only(condition, value):
            return jnp.where(condition, value, 0.0)

        mag[1, 0] = h_x[step, 0] + in_x * (
            sx[0, step, 1] - only(lane2 == last_z, edges[0][:width_y])
        )
        mag[2, 0] = h_x[step, 1] - in_x * (sx[0, step, 0] - only(row2 == last_y, edges[1][0:1]))
        below_y = (
            h_y[step, 0] - in_y * (sy[0, step, 1] - only(lane3 == last_z, edges[2][:width_x])),
            h_y[step, 1] + in_y * (sy[0, step, 0] - only(row3 == last_x, edges[3][0:1])),
        )
        own = sz[0, step]
        for_x = only(lane2 < width_x, pltpu.roll(own, LANES - width_x, 1))
        for_x = for_x - only((row2 == last_y) & (lane2 < width_x), edges[4][0:1])
        for_y = only((lane2 >= width_x) & (lane2 < 2 * width_x), pltpu.roll(own, width_x, 1))
        for_y = for_y - only(lane2 == at, edges[5][:width_y])
        below_z = h_z[step] + in_z * (for_x - for_y)
        above_z = e_z[step]

        cos_h = pick(step, [math.cos(a) for a in angle_h])
        sin_h = pick(step, [math.sin(a) for a in angle_h])
        for x in range(width_x):
            def beyond_y(k):
                return only(row2 == last_y, SPEED * e_y[step, k, x : x + 1, :])

            def beyond_z(k):
                ghost = pltpu.roll(above_z, (LANES - 1 - k * width_x - x) % LANES, 1)
                return only(lane2 == last_z, SPEED * ghost)

            hx = mag[0, x + 1] - beyond_y(1) + beyond_z(1)
            hy = mag[1, x + 1] - beyond_z(0)
            hz = mag[2, x + 1] + beyond_y(0)
            if x == last_x:
                hy = hy + SPEED * e_x[step, 1]
                hz = hz - SPEED * e_x[step, 0]
            mag[0, x + 1] = hx
            mag[1, x + 1] = hy
            mag[2, x + 1] = hz

            def down_y(f, k):
                return jnp.where(row2 == 0, below_y[k][x : x + 1, :], pltpu.roll(f, 1, 0))

            def down_z(f, k):
                ghost = pltpu.roll(below_z, (-k * width_x - x) % LANES, 1)
                return jnp.where(lane2 == 0, ghost, pltpu.roll(f, 1, 1))

            curl = (
                (hz - down_y(hz, 1)) - (hy - down_z(hy, 1)),
                (hx - down_z(hx, 0)) - (hz - mag[2, x]),
                (hy - mag[1, x]) - (hx - down_y(hx, 0)),
            )
            for c in range(3):
                ele[c, x] = ele[c, x] + SPEED * curl[c]
            add_phasors(x, 0, (-cos_h * hz, sin_h * hz, cos_h * hy, -sin_h * hy))
        return carry

    acc[...] = jnp.zeros_like(acc)
    for copy in loads:
        copy.wait()
    lax.fori_loop(0, STEPS, step_body, 0)
    stores = []
    for c in range(3):
        stores.append((ele.at[c, pl.ds(0, width_x)], out_ref.at[c]))
        stores.append((mag.at[c, pl.ds(1, width_x)], out_ref.at[3 + c]))
    stores = [pltpu.make_async_copy(a, b, out_sem.at[k]) for k, (a, b) in enumerate(stores)]
    for copy in stores:
        copy.start()
    add_electric(math.cos(angle_e[-1]), math.sin(angle_e[-1]))

    row_z = lax.broadcasted_iota(jnp.int32, (depth_z, depth_z), 0)
    col_z = lax.broadcasted_iota(jnp.int32, (depth_z, depth_z), 1)
    offset = lax.rem(col_z, half_z)
    mirror = jnp.where(col_z < half_z, 1.0, -1.0)
    fold = jnp.where(row_z == half_z + offset, 1.0, 0.0)
    fold = (fold + jnp.where(row_z == half_z - 1 - offset, mirror, 0.0)).astype(jnp.bfloat16)
    height = folded.shape[1] // 2
    places = [place_ref[0, iz, min(j, slots - 1)] for j in range(height // 8)]
    split = []
    for ty in range(TY):
        rows_ty = jnp.concatenate([acc[:, p, ty, :] for p in places], axis=0).astype(jnp.bfloat16)
        split.append(jnp.dot(rows_ty, fold, preferred_element_type=jnp.float32))
    first_half = lax.broadcasted_iota(jnp.int32, (height, depth_z), 1) < half_z
    for k in range(TY // 2):
        above, under = split[TY // 2 + k], split[TY // 2 - 1 - k]
        same, other = above + under, above - under
        block = pl.ds(k * depth_z, depth_z)
        folded[0, pl.ds(0, height), block] = jnp.where(first_half, same, other).astype(jnp.bfloat16)
        folded[1, pl.ds(0, height), block] = jnp.where(first_half, other, same).astype(jnp.bfloat16)

    partner = {"gy": iy + 1 - 2 * parity}
    to_pair = [
        pltpu.make_async_remote_copy(
            src_ref=source, dst_ref=target,
            send_sem=pair_send.at[k], recv_sem=pair_recv.at[k],
            device_id=partner, device_id_type=MESH,
        )
        for k, (source, target) in enumerate((
            (folded.at[0, pl.ds(0, height)], folded.at[0, pl.ds(height, height)]),
            (folded.at[1, pl.ds(0, height)], folded.at[1, pl.ds(height, height)]),
            (coords.at[0], coords.at[1]),
        ))
    ]
    for copy in to_pair:
        copy.start()

    scale = 1.0 / math.sqrt(n_x * n_y * n_z * TILE_MEAN * TY * depth_z)
    even = lax.rem(lax.broadcasted_iota(jnp.int32, (8, reach), 0), 2) == 0

    def far_copy(o):
        m = lax.rem(me + o, owners)
        return pltpu.make_async_remote_copy(
            src_ref=blocks.at[o], dst_ref=landed.at[o],
            send_sem=far_send.at[o], recv_sem=far_recv.at[o],
            device_id=owner_device(m), device_id_type=MESH,
        )

    def add_tiles(sums, m, first, halves):
        u, v = sums
        ux, uy, uz = dirs[m, 0:1, :], dirs[m, 1:2, :], dirs[m, 2:3, :]
        part = pl.ds(first * height, halves * height)
        in_cos = jnp.dot(folded[0, part], table[m, 0], preferred_element_type=jnp.float32)
        in_sin = jnp.dot(folded[1, part], table[m, 1], preferred_element_type=jnp.float32)
        for half in range(halves):
            at = coords[first + half]
            tc, ts = cos_sin(at[:, 0:1] * ux + at[:, 1:2] * uy + at[:, 2:3] * uz)
            tc, ts = tc * at[:, 3:4], ts * at[:, 3:4]
            for j in range(slots):
                row = half * height + j * 8
                pc, ps = in_cos[row : row + 8], in_sin[row : row + 8]
                c, s = tc[j : j + 1, :], ts[j : j + 1, :]
                u = u + (pc * c - ps * s)
                v = v + (pc * s + ps * c)
        return u, v

    empty = (jnp.zeros((8, reach), jnp.float32), jnp.zeros((8, reach), jnp.float32))

    def keep_block(o, sums):
        u, v = sums
        blocks[o] = jnp.where(even, u - pltpu.roll(v, 7, 0), u + pltpu.roll(v, 1, 0)) * scale

    bunch = next(size for size in (3, 1) if (owners - 1) % size == 0)

    def far_step(i, carry):
        turn = [1 + i * bunch + r for r in range(bunch)]
        all_sums = [add_tiles(empty, lax.rem(me + o, owners), 0, 2) for o in turn]
        for o, sums in zip(turn, all_sums):
            keep_block(o, sums)
            far_copy(o).start()
        return carry

    sums = add_tiles(empty, me, 0, 1)
    for copy in to_pair:
        copy.wait()
    lax.fori_loop(0, (owners - 1) // bunch, far_step, 0)
    keep_block(0, add_tiles(sums, me, 1, 1))

    def gather_step(o, total):
        far_copy(o).wait()
        return total + landed[o]

    total = lax.fori_loop(1, owners, gather_step, blocks[0])
    far_ref[...] = total
    for copy in stores:
        copy.wait()


def hand_out(fields_ref, far_ref, fields_out, far_out, sems):
    pairs = [(fields_ref.at[c], fields_out.at[c]) for c in range(fields_ref.shape[0])]
    pairs.append((far_ref, far_out))
    copies = [pltpu.make_async_copy(a, b, sems.at[k]) for k, (a, b) in enumerate(pairs)]
    for copy in copies:
        copy.start()
    for copy in copies:
        copy.wait()


def shards(
    fields, polarization, material, omega0, damping, strength,
    tile_count, tile_place, dir_angles, dir_order,
):
    sizes = tuple(lax.axis_size(name) for name in ("gx", "gy", "gz"))
    n_x, n_y, n_z = sizes
    devices = n_x * n_y * n_z
    width_x, width_y, depth_z = material.shape
    slots = tile_place.shape[2]
    count = dir_order.shape[0]
    reach = count // devices
    owners = devices // 2
    order = dir_order.reshape(n_x * (n_y // 2), 2, n_z, 1, reach)
    even_slots = slots + slots % 2
    coord_rows = -(-slots // 8) * 8
    f32 = jnp.float32
    anywhere = pl.BlockSpec(memory_space=pl.ANY)
    vmem, smem = pl.BlockSpec(memory_space=pltpu.VMEM), pl.BlockSpec(memory_space=pltpu.SMEM)
    x_face, y_face, z_face = (2, width_y, depth_z), (2, width_x, depth_z), (width_y, LANES)
    fields_out, far = pl.pallas_call(
        functools.partial(kernel, sizes, slots, reach),
        out_shape=(
            jax.ShapeDtypeStruct(fields.shape, f32),
            jax.ShapeDtypeStruct((8, reach), f32),
        ),
        in_specs=[anywhere] * 2 + [vmem] + [smem] * 5 + [vmem] * 2,
        out_specs=(anywhere, vmem),
        scratch_shapes=[
            pltpu.VMEM((3, width_x + 1, width_y, depth_z), f32),
            pltpu.VMEM((3, width_x + 1, width_y, depth_z), f32),
            pltpu.VMEM((2, 3, width_x, width_y, depth_z), f32),
            pltpu.VMEM((4, width_x, width_y, depth_z), f32),
            pltpu.VMEM((8, width_x * width_y // TY, TY, depth_z), f32),
            pltpu.VMEM((2, 2 * even_slots * 8, TY // 2 * depth_z), jnp.bfloat16),
            pltpu.VMEM((2, coord_rows, LANES), f32),
            pltpu.VMEM((2, count // LANES, LANES), f32),
            pltpu.VMEM((2, LANES, 3 * (count // LANES)), jnp.bfloat16),
            pltpu.VMEM((owners, 8, reach), f32),
            pltpu.VMEM((owners, 2, TY // 2 * depth_z, reach), jnp.bfloat16),
            pltpu.VMEM((owners, 8, reach), f32),
            pltpu.VMEM((owners, 8, reach), f32),
        ]
        + [pltpu.VMEM((STEPS,) + face, f32) for face in (x_face, y_face, z_face)] * 2
        + [pltpu.VMEM((STEPS, 6, max(width_x, width_y), LANES), f32)]
        + [pltpu.VMEM((2, STEPS) + face, f32) for face in (x_face, y_face, z_face)]
        + [pltpu.VMEM((STEPS, 6, max(width_x, width_y), LANES), f32)]
        + [
            pltpu.SemaphoreType.DMA((12,)),
            pltpu.SemaphoreType.DMA((STEPS, 12)),
            pltpu.SemaphoreType.DMA((3,)),
            pltpu.SemaphoreType.DMA((3,)),
            pltpu.SemaphoreType.DMA((owners,)),
            pltpu.SemaphoreType.DMA((owners,)),
            pltpu.SemaphoreType.DMA((12,)),
            pltpu.SemaphoreType.DMA((6,)),
        ],
        compiler_params=pltpu.CompilerParams(
            collective_id=0, has_side_effects=True, vmem_limit_bytes=56 * 1024 * 1024
        ),
    )(
        fields, polarization, material, omega0, damping, strength,
        tile_count, tile_place, dir_angles, order,
    )
    fields_out, far = pl.pallas_call(
        hand_out,
        out_shape=(
            jax.ShapeDtypeStruct(fields.shape, f32),
            jax.ShapeDtypeStruct((8, reach), f32),
        ),
        in_specs=[anywhere] * 2,
        out_specs=(anywhere, anywhere),
        scratch_shapes=[pltpu.SemaphoreType.DMA((fields.shape[0] + 1,))],
    )(fields_out, far)
    return fields_out, far.T


def solution(mesh):
    placed = (
        P(None, "gx", "gy", "gz"),
        P(None, "gx", "gy", "gz"),
        P("gx", "gy", "gz"),
        P(),
        P(),
        P(),
        P(("gx", "gy"), None),
        P(("gx", "gy"), None, None),
        P(),
        P(),
    )
    return jax.shard_map(
        shards,
        mesh=mesh,
        in_specs=placed,
        out_specs=(P(None, "gx", "gy", "gz"), P(("gx", "gy", "gz"), None)),
        check_vma=False,
    )
```

```python
import functools
import math

import jax
import jax.numpy as jnp
from jax import lax
from jax.experimental import pallas as pl
from jax.experimental.pallas import tpu as pltpu
from jax.sharding import PartitionSpec as P

TY = 8
STEPS = 4
TILE_MEAN = 6
SPEED = 0.5
WAVE = 0.35
LANES = 128
MESH = pl.DeviceIdType.MESH

SIN_TERMS = (
    6.283185302511505, -41.34170040531808, 81.60513138582216, -76.70301535428969,
    42.02592698929055, -14.899846680245616, 3.238137526404064,
)
COS_TERMS = (
    0.9999999890590243, -19.73920449945407, 64.93911745990263, -85.45013953100009,
    60.16763095180868, -25.967599251355935, 6.528658164931359,
)


def poly(s, terms):
    total = jnp.full_like(s, terms[-1])
    for term in terms[-2::-1]:
        total = total * s + term
    return total


def cos_sin(turns):
    t = turns - jnp.round(turns)
    s = t * t
    return poly(s, COS_TERMS), t * poly(s, SIN_TERMS)


def pick(step, values):
    result = jnp.float32(values[-1])
    for index in range(len(values) - 2, -1, -1):
        result = jnp.where(step == index, jnp.float32(values[index]), result)
    return result


def kernel(
    sizes, slots, reach,
    fields_ref, pol_ref, mat_ref, omega_ref, damp_ref, strength_ref, count_ref, place_ref,
    angles_ref, order_ref,
    out_ref, far_ref,
    ele, mag, pq, coef, acc, folded, coords, spread, parts, dirs, table, blocks, landed,
    e_x, e_y, e_z, h_x, h_y, h_z, edge, sx, sy, sz, edge_out,
    face_send, face_recv, pair_send, pair_recv, far_send, far_recv, in_sem, out_sem,
):
    n_x, n_y, n_z = sizes
    half_y = n_y // 2
    owners = n_x * half_y * n_z
    width_x, width_y, depth_z = mat_ref.shape
    blocks_y = width_y // TY
    ix, iy, iz = lax.axis_index("gx"), lax.axis_index("gy"), lax.axis_index("gz")
    parity = lax.rem(iy, 2)
    me = (ix * half_y + iy // 2) * n_z + iz
    place_in = (("gx", ix, n_x), ("gy", iy, n_y), ("gz", iz, n_z))

    def owner_device(m):
        return {
            "gx": m // (half_y * n_z),
            "gy": lax.rem(m // n_z, half_y) * 2 + parity,
            "gz": lax.rem(m, n_z),
        }

    loads = []
    for c in range(3):
        loads.append((fields_ref.at[c], ele.at[c, pl.ds(0, width_x)]))
        loads.append((fields_ref.at[3 + c], mag.at[c, pl.ds(1, width_x)]))
        loads.append((pol_ref.at[c], pq.at[0, c]))
        loads.append((pol_ref.at[3 + c], pq.at[1, c]))
    loads = [pltpu.make_async_copy(a, b, in_sem.at[k]) for k, (a, b) in enumerate(loads)]
    for copy in loads:
        copy.start()

    for ghost in (e_x, e_y, e_z, h_x, h_y, h_z, edge, edge_out):
        ghost[...] = jnp.zeros_like(ghost)

    barrier = pltpu.get_barrier_semaphore()

    def greet(o, carry):
        pl.semaphore_signal(
            barrier, inc=1, device_id=owner_device(lax.rem(me + o, owners)), device_id_type=MESH
        )
        return carry

    lax.fori_loop(1, owners, greet, 0)

    def exists(offset):
        found = jnp.int32(1)
        for (_, index, count), move in zip(place_in, offset):
            if move:
                found = found * jnp.where((index + move >= 0) & (index + move < count), 1, 0)
        return found

    def device_at(offset):
        return {name: index + move for (name, index, _), move in zip(place_in, offset) if move}

    others = ((0, 1, 0), (0, -1, 0), (1, -1, 0), (-1, 1, 0), (0, 1, -1), (0, -1, 1))
    for offset in others:
        pl.when(exists(offset) > 0)(
            functools.partial(
                pl.semaphore_signal,
                barrier, inc=1, device_id=device_at(offset), device_id_type=MESH,
            )
        )

    material = mat_ref[...]
    coefs = [jnp.zeros(material.shape, jnp.float32) for _ in range(3)]
    for m in range(omega_ref.shape[0]):
        w, g, s = omega_ref[m], damp_ref[m], strength_ref[m]
        w, g, s = (jnp.full((1, 1, depth_z), v, jnp.float32) for v in (w, g, s))
        below = 1.0 + 0.5 * g
        chosen = material == m + 1
        for i, v in enumerate(((2.0 - w * w) / below, -(1.0 - 0.5 * g) / below, s * (w * w) / below)):
            coefs[i] = jnp.where(chosen, v, coefs[i])
    for i in range(3):
        coef[i] = coefs[i]
    coef[3] = jnp.where(material > 0, 1.0, 0.0).astype(jnp.float32)

    first_x, first_y, first_z = ix * width_x, iy * width_y, iz * depth_z
    lane = lax.broadcasted_iota(jnp.int32, (1, LANES), 1)
    coords[0] = jnp.zeros(coords.shape[1:], jnp.float32)
    for j in range(slots):
        p = place_ref[0, iz, j]
        x0 = (first_x + p // blocks_y).astype(jnp.float32)
        y0 = (first_y + lax.rem(p, blocks_y) * TY).astype(jnp.float32)
        z0 = first_z.astype(jnp.float32) + 0.5 * (depth_z - 1)
        live = jnp.where(j < count_ref[0, iz], jnp.float32(1.0), jnp.float32(0.0))
        row = jnp.where(lane == 0, x0, 0.0) + jnp.where(lane == 1, y0 + 0.5 * (TY - 1), 0.0)
        row = row + jnp.where(lane == 2, z0, 0.0) + jnp.where(lane == 3, live, 0.0)
        coords[0, j : j + 1, :] = row

    high_count = spread.shape[1]
    for a in range(2):
        for h in range(high_count):
            spread[a, h : h + 1, :] = angles_ref[a : a + 1, h * LANES : (h + 1) * LANES]
        whole = spread[a]
        part_a = whole.astype(jnp.bfloat16).astype(jnp.float32)
        part_b = (whole - part_a).astype(jnp.bfloat16).astype(jnp.float32)
        part_c = whole - part_a - part_b
        parts[a] = jnp.concatenate([part_a, part_b, part_c], axis=0).T.astype(jnp.bfloat16)

    pl.semaphore_wait(
        barrier,
        owners - 1 + sum(exists(offset) for offset in others),
    )

    half_z = depth_z // 2
    per_turn = WAVE / (2.0 * math.pi)

    def build(m, carry):
        chosen = order_ref[m // n_z, parity, lax.rem(m, n_z)]
        high = lax.rem(lax.broadcasted_iota(jnp.int32, (3 * high_count, reach), 0), high_count)
        low = lax.broadcasted_iota(jnp.int32, (LANES, reach), 0)
        hot = jnp.where(high == chosen // LANES, 1.0, 0.0).astype(jnp.bfloat16)
        own = low == lax.rem(chosen, LANES)
        theta, phi = (
            jnp.sum(
                jnp.where(own, jnp.dot(parts[a], hot, preferred_element_type=jnp.float32), 0.0),
                axis=0,
                keepdims=True,
            )
            for a in range(2)
        )
        ct, st = cos_sin(theta * (1.0 / (2.0 * math.pi)))
        cp, sp = cos_sin(phi * (1.0 / (2.0 * math.pi)))
        ux, uy, uz = st * cp * per_turn, st * sp * per_turn, ct * per_turn
        dirs[m, 0:1, :] = ux
        dirs[m, 1:2, :] = uy
        dirs[m, 2:3, :] = uz
        z_pos = lax.broadcasted_iota(jnp.int32, (half_z, reach), 0).astype(jnp.float32) + 0.5
        zc, zs = cos_sin(uz * z_pos)
        y_pos = lax.broadcasted_iota(jnp.int32, (8, reach), 0).astype(jnp.float32) + 0.5
        yc, ys = cos_sin(uy * y_pos)
        for k in range(TY // 2):
            c, s = yc[k : k + 1, :], ys[k : k + 1, :]
            upper, lower = pl.ds(k * depth_z, half_z), pl.ds(k * depth_z + half_z, half_z)
            table[m, 0, upper, :] = (zc * c).astype(jnp.bfloat16)
            table[m, 0, lower, :] = (zs * -s).astype(jnp.bfloat16)
            table[m, 1, upper, :] = (zc * s).astype(jnp.bfloat16)
            table[m, 1, lower, :] = (zs * c).astype(jnp.bfloat16)
        return carry

    phases = STEPS
    share = -(-owners // phases)
    group = math.gcd(owners // phases, 4) if owners % phases == 0 else 1

    def build_share(phase):
        first = jnp.minimum(phase * share, owners)
        count = jnp.minimum(share, owners - first) // group

        def build_group(i, carry):
            for r in range(group):
                build(first + i * group + r, carry)
            return carry

        lax.fori_loop(0, count, build_group, 0)

    lane2 = lax.broadcasted_iota(jnp.int32, (width_y, LANES), 1)
    row2 = lax.broadcasted_iota(jnp.int32, (width_y, LANES), 0)
    lane3 = lax.broadcasted_iota(jnp.int32, (width_x, LANES), 1)
    row3 = lax.broadcasted_iota(jnp.int32, (width_x, LANES), 0)

    def copies_of(step, group):
        low = ((-1, 0, 0), (0, -1, 0), (0, 0, -1))
        high = ((1, 0, 0), (0, 1, 0), (0, 0, 1))
        across = ((1, 0, -1), (1, -1, 0), (0, 1, -1), (-1, 1, 0), (0, -1, 1), (-1, 0, 1))
        if group == 0:
            ends = [(s.at[0, step], d.at[step]) for s, d in zip((sx, sy, sz), (e_x, e_y, e_z))]
            moves = list(zip(low, ends))
            ends = [(edge_out.at[step, k], edge.at[step, k]) for k in range(6)]
            moves = moves + list(zip(across, ends))
        else:
            ends = [(s.at[1, step], d.at[step]) for s, d in zip((sx, sy, sz), (h_x, h_y, h_z))]
            moves = list(zip(high, ends))
        result = []
        for k, (offset, (source, target)) in enumerate(moves):
            copy = pltpu.make_async_remote_copy(
                src_ref=source,
                dst_ref=target,
                send_sem=face_send.at[group * 9 + k],
                recv_sem=face_recv.at[step, group * 9 + k],
                device_id=device_at(offset),
                device_id_type=MESH,
            )
            result.append((exists(offset) > 0, exists(tuple(-m for m in offset)) > 0, copy))
        return result

    def start_all(copies):
        for sends, _, copy in copies:
            pl.when(sends)(copy.start)

    def wait_all(copies):
        for sends, receives, copy in copies:
            pl.when(sends)(copy.wait_send)
            pl.when(receives)(copy.wait_recv)

    def pack_z(pairs, from_lane):
        total = jnp.zeros((width_y, LANES), jnp.float32)
        for k, plane in enumerate(pairs):
            for x in range(width_x):
                at = k * width_x + x
                rolled = pltpu.roll(plane(x), (at - from_lane) % LANES, 1)
                total = jnp.where(lane2 == at, rolled, total)
        return total

    def add_phasors(x, first, terms):
        for c, term in enumerate(terms):
            for k in range(blocks_y):
                at = x * blocks_y + k
                acc[first + c, at] = acc[first + c, at] + term[k * TY : (k + 1) * TY]

    def add_electric(cos_e, sin_e):
        for x in range(width_x):
            ey, ez = ele[1, x], ele[2, x]
            add_phasors(x, 4, (cos_e * ez, -sin_e * ez, -cos_e * ey, sin_e * ey))

    angle_h = [WAVE * SPEED * (n + 0.5) for n in range(STEPS)]
    angle_e = [WAVE * SPEED * (n + 1.0) for n in range(STEPS)]

    def step_body(step, carry):
        now, old = lax.rem(step, 2), lax.rem(step + 1, 2)
        sx[0, step, 0] = ele[1, 0]
        sx[0, step, 1] = ele[2, 0]
        sy[0, step, 0] = ele[0, pl.ds(0, width_x), 0, :]
        sy[0, step, 1] = ele[2, pl.ds(0, width_x), 0, :]
        sz[0, step] = pack_z((lambda x: ele[0, x], lambda x: ele[1, x]), 0)
        last_x, last_y, last_z = width_x - 1, width_y - 1, depth_z - 1
        edge_out[step, 0, pl.ds(0, width_y)] = pltpu.roll(ele[0, last_x], last_z, 1)
        edge_out[step, 1, 0:1] = ele[0, last_x, 0:1, :]
        edge_out[step, 2, pl.ds(0, width_x)] = pltpu.roll(ele[1, pl.ds(0, width_x), last_y, :], last_z, 1)
        edge_out[step, 3, 0:1] = ele[1, 0, last_y : last_y + 1, :]
        edge_out[step, 4, 0:1] = pack_z((lambda x: ele[2, x],), last_z)[0:1]
        at = 2 * width_x - 1
        edge_out[step, 5, pl.ds(0, width_y)] = pltpu.roll(ele[2, 0], (at - last_z) % LANES, 1)
        electric_copies = copies_of(step, 0)
        start_all(electric_copies)

        for x in range(width_x):
            ex, ey, ez = ele[0, x], ele[1, x], ele[2, x]

            def up_y(f):
                return jnp.where(row2 == last_y, 0.0, pltpu.roll(f, last_y, 0))

            def up_z(f):
                return jnp.where(lane2 == last_z, 0.0, pltpu.roll(f, last_z, 1))

            ahead_y = ele[1, x + 1] if x < last_x else jnp.zeros_like(ey)
            ahead_z = ele[2, x + 1] if x < last_x else jnp.zeros_like(ez)
            mag[0, x + 1] = mag[0, x + 1] - SPEED * ((up_y(ez) - ez) - (up_z(ey) - ey))
            mag[1, x + 1] = mag[1, x + 1] - SPEED * ((up_z(ex) - ex) - (ahead_z - ez))
            mag[2, x + 1] = mag[2, x + 1] - SPEED * ((ahead_y - ey) - (up_y(ex) - ex))
        sx[1, step, 0] = mag[1, width_x]
        sx[1, step, 1] = mag[2, width_x]
        sy[1, step, 0] = mag[0, pl.ds(1, width_x), last_y, :]
        sy[1, step, 1] = mag[2, pl.ds(1, width_x), last_y, :]
        sz[1, step] = pack_z((lambda x: mag[0, x + 1], lambda x: mag[1, x + 1]), last_z)
        magnetic_copies = copies_of(step, 1)
        start_all(magnetic_copies)

        build_share(step)
        add_electric(
            pick(step, [0.0] + [math.cos(a) for a in angle_e[:-1]]),
            pick(step, [0.0] + [math.sin(a) for a in angle_e[:-1]]),
        )
        for x in range(width_x):
            e = [ele[c, x] for c in range(3)]
            sat = 1.0 / (1.0 + e[0] * e[0] + e[1] * e[1] + e[2] * e[2])
            a, b, strength, sheet = coef[0, x], coef[1, x], coef[2, x] * sat, coef[3, x]
            for c in range(3):
                p = pq[now, c, x]
                pn = a * p + b * pq[old, c, x] + strength * e[c]
                pq[old, c, x] = pn
                ele[c, x] = e[c] - sheet * (pn - p)
        wait_all(electric_copies)
        wait_all(magnetic_copies)

        in_x, in_y, in_z = (
            jnp.where(index > 0, jnp.float32(SPEED), jnp.float32(0.0)) for _, index, _ in place_in
        )
        edges = [edge[step, k] for k in range(6)]

        def only(condition, value):
            return jnp.where(condition, value, 0.0)

        mag[1, 0] = h_x[step, 0] + in_x * (
            sx[0, step, 1] - only(lane2 == last_z, edges[0][:width_y])
        )
        mag[2, 0] = h_x[step, 1] - in_x * (sx[0, step, 0] - only(row2 == last_y, edges[1][0:1]))
        below_y = (
            h_y[step, 0] - in_y * (sy[0, step, 1] - only(lane3 == last_z, edges[2][:width_x])),
            h_y[step, 1] + in_y * (sy[0, step, 0] - only(row3 == last_x, edges[3][0:1])),
        )
        own = sz[0, step]
        for_x = only(lane2 < width_x, pltpu.roll(own, LANES - width_x, 1))
        for_x = for_x - only((row2 == last_y) & (lane2 < width_x), edges[4][0:1])
        for_y = only((lane2 >= width_x) & (lane2 < 2 * width_x), pltpu.roll(own, width_x, 1))
        for_y = for_y - only(lane2 == at, edges[5][:width_y])
        below_z = h_z[step] + in_z * (for_x - for_y)
        above_z = e_z[step]

        cos_h = pick(step, [math.cos(a) for a in angle_h])
        sin_h = pick(step, [math.sin(a) for a in angle_h])
        for x in range(width_x):
            def beyond_y(k):
                return only(row2 == last_y, SPEED * e_y[step, k, x : x + 1, :])

            def beyond_z(k):
                ghost = pltpu.roll(above_z, (LANES - 1 - k * width_x - x) % LANES, 1)
                return only(lane2 == last_z, SPEED * ghost)

            hx = mag[0, x + 1] - beyond_y(1) + beyond_z(1)
            hy = mag[1, x + 1] - beyond_z(0)
            hz = mag[2, x + 1] + beyond_y(0)
            if x == last_x:
                hy = hy + SPEED * e_x[step, 1]
                hz = hz - SPEED * e_x[step, 0]
            mag[0, x + 1] = hx
            mag[1, x + 1] = hy
            mag[2, x + 1] = hz

            def down_y(f, k):
                return jnp.where(row2 == 0, below_y[k][x : x + 1, :], pltpu.roll(f, 1, 0))

            def down_z(f, k):
                ghost = pltpu.roll(below_z, (-k * width_x - x) % LANES, 1)
                return jnp.where(lane2 == 0, ghost, pltpu.roll(f, 1, 1))

            curl = (
                (hz - down_y(hz, 1)) - (hy - down_z(hy, 1)),
                (hx - down_z(hx, 0)) - (hz - mag[2, x]),
                (hy - mag[1, x]) - (hx - down_y(hx, 0)),
            )
            for c in range(3):
                ele[c, x] = ele[c, x] + SPEED * curl[c]
            add_phasors(x, 0, (-cos_h * hz, sin_h * hz, cos_h * hy, -sin_h * hy))
        return carry

    acc[...] = jnp.zeros_like(acc)
    for copy in loads:
        copy.wait()
    lax.fori_loop(0, STEPS, step_body, 0)
    stores = []
    for c in range(3):
        stores.append((ele.at[c, pl.ds(0, width_x)], out_ref.at[c]))
        stores.append((mag.at[c, pl.ds(1, width_x)], out_ref.at[3 + c]))
    stores = [pltpu.make_async_copy(a, b, out_sem.at[k]) for k, (a, b) in enumerate(stores)]
    for copy in stores:
        copy.start()
    add_electric(math.cos(angle_e[-1]), math.sin(angle_e[-1]))

    row_z = lax.broadcasted_iota(jnp.int32, (depth_z, depth_z), 0)
    col_z = lax.broadcasted_iota(jnp.int32, (depth_z, depth_z), 1)
    offset = lax.rem(col_z, half_z)
    mirror = jnp.where(col_z < half_z, 1.0, -1.0)
    fold = jnp.where(row_z == half_z + offset, 1.0, 0.0)
    fold = (fold + jnp.where(row_z == half_z - 1 - offset, mirror, 0.0)).astype(jnp.bfloat16)
    height = folded.shape[1] // 2
    places = [place_ref[0, iz, min(j, slots - 1)] for j in range(height // 8)]
    split = []
    for ty in range(TY):
        rows_ty = jnp.concatenate([acc[:, p, ty, :] for p in places], axis=0).astype(jnp.bfloat16)
        split.append(jnp.dot(rows_ty, fold, preferred_element_type=jnp.float32))
    first_half = lax.broadcasted_iota(jnp.int32, (height, depth_z), 1) < half_z
    for k in range(TY // 2):
        above, under = split[TY // 2 + k], split[TY // 2 - 1 - k]
        same, other = above + under, above - under
        block = pl.ds(k * depth_z, depth_z)
        folded[0, pl.ds(0, height), block] = jnp.where(first_half, same, other).astype(jnp.bfloat16)
        folded[1, pl.ds(0, height), block] = jnp.where(first_half, other, same).astype(jnp.bfloat16)

    partner = {"gy": iy + 1 - 2 * parity}
    to_pair = [
        pltpu.make_async_remote_copy(
            src_ref=source, dst_ref=target,
            send_sem=pair_send.at[k], recv_sem=pair_recv.at[k],
            device_id=partner, device_id_type=MESH,
        )
        for k, (source, target) in enumerate((
            (folded.at[0, pl.ds(0, height)], folded.at[0, pl.ds(height, height)]),
            (folded.at[1, pl.ds(0, height)], folded.at[1, pl.ds(height, height)]),
            (coords.at[0], coords.at[1]),
        ))
    ]
    for copy in to_pair:
        copy.start()

    scale = 1.0 / math.sqrt(n_x * n_y * n_z * TILE_MEAN * TY * depth_z)
    even = lax.rem(lax.broadcasted_iota(jnp.int32, (8, reach), 0), 2) == 0

    def far_copy(o):
        m = lax.rem(me + o, owners)
        return pltpu.make_async_remote_copy(
            src_ref=blocks.at[o], dst_ref=landed.at[o],
            send_sem=far_send.at[o], recv_sem=far_recv.at[o],
            device_id=owner_device(m), device_id_type=MESH,
        )

    def add_tiles(sums, m, first, halves):
        u, v = sums
        ux, uy, uz = dirs[m, 0:1, :], dirs[m, 1:2, :], dirs[m, 2:3, :]
        part = pl.ds(first * height, halves * height)
        in_cos = jnp.dot(folded[0, part], table[m, 0], preferred_element_type=jnp.float32)
        in_sin = jnp.dot(folded[1, part], table[m, 1], preferred_element_type=jnp.float32)
        for half in range(halves):
            at = coords[first + half]
            tc, ts = cos_sin(at[:, 0:1] * ux + at[:, 1:2] * uy + at[:, 2:3] * uz)
            tc, ts = tc * at[:, 3:4], ts * at[:, 3:4]
            for j in range(slots):
                row = half * height + j * 8
                pc, ps = in_cos[row : row + 8], in_sin[row : row + 8]
                c, s = tc[j : j + 1, :], ts[j : j + 1, :]
                u = u + (pc * c - ps * s)
                v = v + (pc * s + ps * c)
        return u, v

    empty = (jnp.zeros((8, reach), jnp.float32), jnp.zeros((8, reach), jnp.float32))

    def keep_block(o, sums):
        u, v = sums
        blocks[o] = jnp.where(even, u - pltpu.roll(v, 7, 0), u + pltpu.roll(v, 1, 0)) * scale

    bunch = next(size for size in (3, 1) if (owners - 1) % size == 0)

    def far_step(i, carry):
        turn = [1 + i * bunch + r for r in range(bunch)]
        all_sums = [add_tiles(empty, lax.rem(me + o, owners), 0, 2) for o in turn]
        for o, sums in zip(turn, all_sums):
            keep_block(o, sums)
            far_copy(o).start()
        return carry

    sums = add_tiles(empty, me, 0, 1)
    for copy in to_pair:
        copy.wait()
    lax.fori_loop(0, (owners - 1) // bunch, far_step, 0)
    keep_block(0, add_tiles(sums, me, 1, 1))

    def gather_step(o, total):
        far_copy(o).wait()
        return total + landed[o]

    total = lax.fori_loop(1, owners, gather_step, blocks[0])
    far_ref[...] = total
    for copy in stores:
        copy.wait()


def shards(
    fields, polarization, material, omega0, damping, strength,
    tile_count, tile_place, dir_angles, dir_order,
):
    sizes = tuple(lax.axis_size(name) for name in ("gx", "gy", "gz"))
    n_x, n_y, n_z = sizes
    devices = n_x * n_y * n_z
    width_x, width_y, depth_z = material.shape
    slots = tile_place.shape[2]
    count = dir_order.shape[0]
    reach = count // devices
    owners = devices // 2
    order = dir_order.reshape(n_x * (n_y // 2), 2, n_z, 1, reach)
    even_slots = slots + slots % 2
    coord_rows = -(-slots // 8) * 8
    f32 = jnp.float32
    anywhere = pl.BlockSpec(memory_space=pl.ANY)
    vmem, smem = pl.BlockSpec(memory_space=pltpu.VMEM), pl.BlockSpec(memory_space=pltpu.SMEM)
    x_face, y_face, z_face = (2, width_y, depth_z), (2, width_x, depth_z), (width_y, LANES)
    fields_out, far = pl.pallas_call(
        functools.partial(kernel, sizes, slots, reach),
        out_shape=(
            jax.ShapeDtypeStruct(fields.shape, f32),
            jax.ShapeDtypeStruct((8, reach), f32),
        ),
        in_specs=[anywhere] * 2 + [vmem] + [smem] * 5 + [vmem] * 2,
        out_specs=(anywhere, vmem),
        scratch_shapes=[
            pltpu.VMEM((3, width_x + 1, width_y, depth_z), f32),
            pltpu.VMEM((3, width_x + 1, width_y, depth_z), f32),
            pltpu.VMEM((2, 3, width_x, width_y, depth_z), f32),
            pltpu.VMEM((4, width_x, width_y, depth_z), f32),
            pltpu.VMEM((8, width_x * width_y // TY, TY, depth_z), f32),
            pltpu.VMEM((2, 2 * even_slots * 8, TY // 2 * depth_z), jnp.bfloat16),
            pltpu.VMEM((2, coord_rows, LANES), f32),
            pltpu.VMEM((2, count // LANES, LANES), f32),
            pltpu.VMEM((2, LANES, 3 * (count // LANES)), jnp.bfloat16),
            pltpu.VMEM((owners, 8, reach), f32),
            pltpu.VMEM((owners, 2, TY // 2 * depth_z, reach), jnp.bfloat16),
            pltpu.VMEM((owners, 8, reach), f32),
            pltpu.VMEM((owners, 8, reach), f32),
        ]
        + [pltpu.VMEM((STEPS,) + face, f32) for face in (x_face, y_face, z_face)] * 2
        + [pltpu.VMEM((STEPS, 6, max(width_x, width_y), LANES), f32)]
        + [pltpu.VMEM((2, STEPS) + face, f32) for face in (x_face, y_face, z_face)]
        + [pltpu.VMEM((STEPS, 6, max(width_x, width_y), LANES), f32)]
        + [
            pltpu.SemaphoreType.DMA((12,)),
            pltpu.SemaphoreType.DMA((STEPS, 12)),
            pltpu.SemaphoreType.DMA((3,)),
            pltpu.SemaphoreType.DMA((3,)),
            pltpu.SemaphoreType.DMA((owners,)),
            pltpu.SemaphoreType.DMA((owners,)),
            pltpu.SemaphoreType.DMA((12,)),
            pltpu.SemaphoreType.DMA((6,)),
        ],
        compiler_params=pltpu.CompilerParams(
            collective_id=0, has_side_effects=True, vmem_limit_bytes=56 * 1024 * 1024
        ),
    )(
        fields, polarization, material, omega0, damping, strength,
        tile_count, tile_place, dir_angles, order,
    )
    return fields_out, far.T


def solution(mesh):
    placed = (
        P(None, "gx", "gy", "gz"),
        P(None, "gx", "gy", "gz"),
        P("gx", "gy", "gz"),
        P(),
        P(),
        P(),
        P(("gx", "gy"), None),
        P(("gx", "gy"), None, None),
        P(),
        P(),
    )
    return jax.shard_map(
        shards,
        mesh=mesh,
        in_specs=placed,
        out_specs=(P(None, "gx", "gy", "gz"), P(("gx", "gy", "gz"), None)),
        check_vma=False,
    )
```
